512 devices in a mesh: expert: 128 (over z_hi, x, y), dp: 4 (over z_lo, core).
Axes of the slice: x: 4, y: 8, z: 8 (z_hi: 4, z_lo: 2; z = z_hi * 2 + z_lo), core: 2. Of those that a mesh axis runs over, the one named last changes fastest.
Arguments:
- tokens: bfloat16 [512, 128, 1280], P(('expert', 'dp')), may hold values from -26 to 26
- grad_out: bfloat16 [512, 128, 1280], P(('expert', 'dp')), may hold values from -6 to 6
- router: bfloat16 [1280, 64], replicated, may hold values from -26 to 26
- up_weight: bfloat16 [128, 1280, 1536], P('expert', None, 'dp'), may hold values from -0.15625 to 0.15625
- down_weight: bfloat16 [128, 1280, 1536], P('expert', None, 'dp'), may hold values from -0.109375 to 0.109375
Outputs:
- grad_tokens: bfloat16 [512, 128, 1280], P(('expert', 'dp'))
- grad_router: float32 [1280, 64], P('dp')
- grad_up: bfloat16 [128, 1280, 1536], P('expert', None, 'dp')
- grad_down: bfloat16 [128, 1280, 1536], P('expert', None, 'dp')
The draws below stay inside these ranges and needn't reach their ends.
All inputs are finite; a program needn't handle non-finite values.
Results may differ from the reference program's by a relative error of at most 0.035.
Values may be sent and summed in bfloat16 or wider, within the bound.
A program may use at most 64 MiB of HBM per device.

```python
import jax
import jax.numpy as jnp
from jax import lax

D = 1280
HID = 3072
TOK = 128
EXPERTS = 64
IMAGES = 512
HALF = 1536
N_EXPERT = 128
N_DP = 4


def draw_tokens(key, part):
    key = jax.random.fold_in(key, 11)
    first, second, third = jax.random.split(key, 3)
    base = jax.random.truncated_normal(first, -4.0, 4.0, (IMAGES, TOK, D), jnp.float32)
    spread = 1.15
    row_scale = jnp.exp(jax.random.uniform(second, (IMAGES, TOK, 1), jnp.float32, -spread, spread))
    col_scale = jnp.exp(jax.random.uniform(third, (1, 1, D), jnp.float32, -0.7, 0.7))
    return (base * row_scale * col_scale).astype(jnp.bfloat16)


def draw_router(key, part):
    key = jax.random.fold_in(key, 23)
    first, second, third = jax.random.split(key, 3)
    base = jax.random.truncated_normal(first, -4.0, 4.0, (D, EXPERTS), jnp.float32)
    spread = 1.15
    col_scale = jnp.exp(jax.random.uniform(second, (1, EXPERTS), jnp.float32, -spread, spread))
    row_scale = jnp.exp(jax.random.uniform(third, (D, 1), jnp.float32, -0.7, 0.7))
    return (base * row_scale * col_scale).astype(jnp.bfloat16)


def block_levels(key, shape, shards, low, high):
    def one(axis_at, blocks):
        draws = jax.random.uniform(jax.random.fold_in(jax.random.fold_in(key, 6), axis_at), (blocks,), jnp.float32, low / len(shards), high / len(shards))
        return jnp.repeat(jnp.exp(draws), shape[axis_at] // blocks).reshape((-1,) + (1,) * (len(shape) - axis_at - 1))

    level = one(*shards[0])
    for cut in shards[1:]:
        level = level * one(*cut)
    return level


def centred(stream_key, shape, deviation, reach, cuts=(), dtype=jnp.bfloat16):
    factor_of = block_levels(stream_key, shape, cuts, -0.22, 0.18) if cuts else 1.0
    drawn = jax.random.normal(stream_key, shape, jnp.float32) * deviation * factor_of
    return jnp.minimum(jnp.maximum(drawn, -reach), reach).astype(dtype)


def setup_inputs(seed: int = 0) -> dict:
    key_of = jax.random.split(jax.random.key(seed), 6)
    tokens = draw_tokens(jax.random.fold_in(key_of[5], 71), 0)
    grad_out = centred(key_of[1], (IMAGES, TOK, D), 1.0, 6.0, ((0, 512),))
    router = draw_router(jax.random.fold_in(key_of[5], 71), 0)
    up_weight = centred(key_of[3], (N_EXPERT, D, HALF), D ** -0.5, 0.15625, ((0, 128), (2, 4)))
    down_weight = centred(key_of[4], (N_EXPERT, D, HALF), HID ** -0.5, 0.109375, ((0, 128), (2, 4)))
    return dict(tokens=tokens, grad_out=grad_out, router=router, up_weight=up_weight, down_weight=down_weight)


logit_scale = 24.0

def exact_gelu(value):
    return jax.nn.gelu(value, approximate=False)

def front(image, router32):
    xf = image.astype(jnp.float32)
    x_norm = xf * lax.rsqrt(lax.optimization_barrier(jnp.sum(xf * xf, axis=1, keepdims=True)) + 1e-06)
    r_norm = router32 * lax.rsqrt(lax.optimization_barrier(jnp.sum(router32 * router32, axis=0, keepdims=True)) + 1e-06)
    logits = logit_scale * jnp.dot(x_norm, r_norm, precision=lax.Precision.HIGHEST)
    weights = jnp.exp(logits)
    dispatch = (weights / lax.optimization_barrier(jnp.sum(weights, axis=0, keepdims=True))).astype(jnp.bfloat16)
    combine = (weights / lax.optimization_barrier(jnp.sum(weights, axis=1, keepdims=True))).astype(jnp.bfloat16)
    slots_in = jnp.dot(dispatch.T, image, preferred_element_type=jnp.float32).astype(jnp.bfloat16)
    return (slots_in, combine)

def piece_sum(left, weight):
    pieces = 2 * N_DP
    left_split = left.astype(jnp.float32).reshape(left.shape[0], pieces, left.shape[1] // pieces)
    weight_split = weight.astype(jnp.float32).reshape(weight.shape[0], pieces, weight.shape[1] // pieces)
    parts = jnp.einsum('rpk,dpk->prd', left_split, weight_split).astype(jnp.bfloat16)
    parts = lax.optimization_barrier(parts)
    return lax.optimization_barrier(jnp.sum(parts.astype(jnp.float32), axis=0)).astype(jnp.bfloat16)

def expert_forward(operands):
    rows, w_up, w_down = operands
    pre = jnp.dot(rows.astype(jnp.float32), w_up.astype(jnp.float32))
    act = exact_gelu(pre).astype(jnp.bfloat16)
    return piece_sum(act, w_down)

def expert_backward(operands):
    rows, grads, w_up, w_down = operands
    pre = jnp.dot(rows.astype(jnp.float32), w_up.astype(jnp.float32))
    act_full, gelu_back = jax.vjp(exact_gelu, pre)
    act = act_full.astype(jnp.bfloat16)
    grads32 = grads.astype(jnp.float32)
    grad_act = jnp.dot(grads32, w_down.astype(jnp.float32))
    grad_pre = gelu_back(grad_act)[0].astype(jnp.bfloat16)
    grad_down_e = jnp.dot(grads32.T, act.astype(jnp.float32)).astype(jnp.bfloat16)
    grad_up_e = jnp.dot(rows.astype(jnp.float32).T, grad_pre.astype(jnp.float32)).astype(jnp.bfloat16)
    return (grad_up_e, grad_down_e, piece_sum(grad_pre, w_up))

def pair_halves(weight):
    return weight.reshape(EXPERTS, 2, D, HALF).transpose(0, 2, 1, 3).reshape(EXPERTS, D, HID)

def split_halves(weight):
    return weight.reshape(EXPERTS, D, 2, HALF).transpose(0, 2, 1, 3).reshape(N_EXPERT, D, HALF)

def reference(tokens, grad_out, router, up_weight, down_weight):
    router32 = router.astype(jnp.float32)
    (slots_in, combine), front_back = jax.vjp(jax.vmap(front, in_axes=(0, None)), tokens, router32)
    slot_rows = jnp.transpose(slots_in, (1, 0, 2))
    up_pairs = pair_halves(up_weight)
    down_pairs = pair_halves(down_weight)
    slots_out = lax.map(expert_forward, (slot_rows, up_pairs, down_pairs))
    slots_out_t = jnp.transpose(slots_out, (1, 0, 2)).astype(jnp.float32)
    grad32 = grad_out.astype(jnp.float32)
    grad_combine = jnp.einsum('itd,isd->its', grad32, slots_out_t).astype(jnp.bfloat16)
    grad_slots_out = jnp.einsum('its,itd->isd', combine.astype(jnp.float32), grad32).astype(jnp.bfloat16)
    grad_up_p, grad_down_p, grad_rows = lax.map(expert_backward, (slot_rows, jnp.transpose(grad_slots_out, (1, 0, 2)), up_pairs, down_pairs))
    grad_slots_in = jnp.transpose(grad_rows, (1, 0, 2))
    grad_tokens, grad_router = front_back((grad_slots_in, grad_combine))
    return (grad_tokens, grad_router.astype(jnp.float32), split_halves(grad_up_p), split_halves(grad_down_p))
```

```python
import jax
import jax.numpy as jnp
from jax import lax
from jax.sharding import PartitionSpec as P

logit_scale = 24.0
f32 = jnp.float32
bf16 = jnp.bfloat16


def exact_gelu(value):
    return jax.nn.gelu(value, approximate=False)


def dot(a, b, ca, cb):
    return lax.dot_general(a, b, (((ca,), (cb,)), ((), ())), preferred_element_type=f32)


def front(x, go, rt):
    xf = x.astype(f32)
    rf = rt.astype(f32)
    inv_x = lax.rsqrt(jnp.sum(xf * xf, axis=1, keepdims=True) + 1e-06)
    inv_r = lax.rsqrt(jnp.sum(rf * rf, axis=1, keepdims=True) + 1e-06).T
    logits = (logit_scale * inv_x) * inv_r * dot(x, rt, 1, 1)
    e = jnp.exp(logits)
    disp = e / jnp.sum(e, axis=0, keepdims=True)
    comb = e / jnp.sum(e, axis=1, keepdims=True)
    slots = dot(disp.astype(bf16), x, 0, 0).astype(bf16)
    grads = dot(comb.astype(bf16), go, 0, 0).astype(bf16)
    return inv_x, inv_r, logits, disp, comb, slots, grads


def back(x, go, rt, saved, slots_out, grad_slots):
    inv_x, inv_r, logits, disp, comb = saved
    d_comb = dot(go, slots_out, 1, 1).astype(bf16).astype(f32)
    d_disp = dot(x, grad_slots, 1, 1).astype(bf16).astype(f32)
    d_log = disp * (d_disp - jnp.sum(disp * d_disp, axis=0, keepdims=True)) + comb * (
        d_comb - jnp.sum(comb * d_comb, axis=1, keepdims=True)
    )
    m = d_log * logits
    row = jnp.sum(m, axis=1, keepdims=True)
    col = jnp.sum(m, axis=0, keepdims=True)
    a = (logit_scale * inv_x) * inv_r * d_log
    hi = a.astype(bf16)
    lo = (a - hi.astype(f32)).astype(bf16)
    left = jnp.concatenate([disp.astype(bf16), hi, lo], axis=1)
    right = jnp.concatenate([grad_slots, rt, rt], axis=0)
    grad_x = dot(left, right, 1, 0) - x.astype(f32) * (inv_x * inv_x * row)
    term = dot(jnp.concatenate([hi, lo], axis=1), x, 0, 0)
    term = term[:64] + term[64:] - rt.astype(f32) * (inv_r * inv_r * col).T
    return grad_x.astype(bf16), term


def local(tokens, grad_out, router, up_weight, down_weight):
    x, go, rt = tokens[0], grad_out[0], router.T
    w_up, w_down = up_weight[0], down_weight[0]
    *saved, slots, grads = front(x, go, rt)
    both = jnp.stack([slots, grads], axis=1)
    sent = jnp.repeat(both, 2, axis=0)
    got = lax.all_to_all(sent, "expert", split_axis=0, concat_axis=0, tiled=True)
    rows = lax.all_gather(got[:, 0], "dp", axis=0, tiled=True)
    grows = lax.all_gather(got[:, 1], "dp", axis=0, tiled=True)
    pre = dot(rows, w_up, 1, 0)
    act, gelu_back = jax.vjp(exact_gelu, pre)
    act = act.astype(bf16)
    grad_act = dot(grows, w_down, 1, 0)
    grad_pre = gelu_back(grad_act)[0].astype(bf16)
    part_y = dot(act, w_down, 1, 1).astype(bf16)
    part_x = dot(grad_pre, w_up, 1, 1).astype(bf16)
    y = lax.psum_scatter(part_y, "dp", scatter_dimension=0, tiled=True)
    dx = lax.psum_scatter(part_x, "dp", scatter_dimension=0, tiled=True)
    grad_down = dot(grows, act, 0, 0).astype(bf16)
    grad_up = dot(rows, grad_pre, 0, 0).astype(bf16)
    back_rows = lax.all_to_all(
        jnp.stack([y, dx], axis=1), "expert", split_axis=0, concat_axis=0, tiled=True
    )
    summed = jnp.sum(back_rows.reshape(64, 2, 2, -1).astype(f32), axis=1).astype(bf16)
    grad_x, term = back(x, go, rt, saved, summed[:, 0], summed[:, 1])
    n_dp, n_ex = lax.axis_size("dp"), lax.axis_size("expert")
    pieces = term.astype(bf16).reshape(64, n_dp, -1).transpose(1, 0, 2)
    pieces = pieces.reshape(n_dp, n_ex, -1)
    own = jnp.sum(lax.all_to_all(pieces, "dp", 0, 0, tiled=True).astype(f32), axis=0)
    own = lax.all_to_all(own.astype(bf16), "expert", 0, 0, tiled=True)
    own = jnp.sum(own.astype(f32), axis=0).astype(bf16)
    whole = lax.all_to_all(jnp.broadcast_to(own, (n_ex, own.shape[0])), "expert", 0, 0, tiled=True)
    router_grad = whole.reshape(64, -1).T.astype(f32)
    return (grad_x[None], router_grad, grad_up[None], grad_down[None])


def solution(mesh):
    placed = (
        P(("expert", "dp"), None, None),
        P(("expert", "dp"), None, None),
        P(),
        P("expert", None, "dp"),
        P("expert", None, "dp"),
    )
    return jax.shard_map(
        local,
        mesh=mesh,
        in_specs=placed,
        out_specs=(
            P(("expert", "dp"), None, None),
            P("dp", None),
            P("expert", None, "dp"),
            P("expert", None, "dp"),
        ),
        check_vma=False,
    )
```

```python
import functools

import jax
import jax.numpy as jnp
from jax import lax
from jax.experimental import pallas as pl
from jax.experimental.pallas import tpu as pltpu
from jax.sharding import PartitionSpec as P

logit_scale = 24.0
f32 = jnp.float32
bf16 = jnp.bfloat16
MESH = pl.DeviceIdType.MESH
N = 8
D = 1280
K = 384
HALF_D = 640


def dot(a, b, ca, cb):
    return lax.dot_general(a, b, (((ca,), (cb,)), ((), ())), preferred_element_type=f32)


def expert_of(k, j):
    return (j // 2) * 16 + (j % 2) * 2 + (k // 2) * 4 + k % 2


def k_of(e):
    return ((e // 4) % 4) * 2 + e % 2


def j_of(e):
    return (e // 16) * 2 + (e % 4) // 2


def pick(source):
    rows = lax.broadcasted_iota(jnp.int32, (128, 128), 0)
    cols = lax.broadcasted_iota(jnp.int32, (128, 128), 1)
    return jnp.where(source(rows) == cols, 1.0, 0.0).astype(bf16)


def by_member(o):
    k, h, j = o >> 4, (o >> 3) & 1, o & 7
    return h * 64 + (j >> 1) * 16 + (j & 1) * 2 + (k >> 1) * 4 + (k & 1)


def by_expert(o):
    h, e = o >> 6, o & 63
    k = ((e >> 2) & 3) * 2 + (e & 1)
    j = (e >> 4) * 2 + ((e >> 1) & 1)
    return k * 16 + h * 8 + j


def swapped(o):
    return (o & 7) * 16 + ((o >> 3) & 1) * 8 + (o >> 4)


def halves_out(o):
    return ((o >> 3) & 7) * 16 + (o >> 6) * 8 + (o & 7)


def halves_in(o):
    return ((o >> 3) & 1) * 64 + (o >> 4) * 8 + (o & 7)


def moved(source, value):
    return dot(pick(source), value, 1, 0).astype(bf16)


def to_row(column):
    return jnp.broadcast_to(column, (128, 128)).T[0:1, :]


def to_column(row):
    return jnp.broadcast_to(row, (128, 128)).T[:, 0:1]


def front(x, go, rt):
    xf = x.astype(f32)
    rf = rt.astype(f32)
    inv_x = to_row(lax.rsqrt(jnp.sum(xf * xf, axis=1, keepdims=True) + 1e-06))
    inv_r = lax.rsqrt(jnp.sum(rf * rf, axis=1, keepdims=True) + 1e-06)
    logits = (logit_scale * inv_x) * inv_r * dot(rt, x, 1, 1)
    e = jnp.exp(logits)
    disp = e / jnp.sum(e, axis=1, keepdims=True)
    comb = e / jnp.sum(e, axis=0, keepdims=True)
    slots = dot(disp.astype(bf16), x, 1, 0).astype(bf16)
    grads = dot(comb.astype(bf16), go, 1, 0).astype(bf16)
    return inv_x, inv_r, logits, disp, comb, slots, grads


def back(x, go, rt, saved, slots_out, grad_slots):
    inv_x, inv_r, logits, disp, comb = saved
    d_comb = dot(slots_out, go, 1, 1).astype(bf16).astype(f32)
    d_disp = dot(grad_slots, x, 1, 1).astype(bf16).astype(f32)
    d_log = disp * (d_disp - jnp.sum(disp * d_disp, axis=1, keepdims=True)) + comb * (
        d_comb - jnp.sum(comb * d_comb, axis=0, keepdims=True)
    )
    m = d_log * logits
    row = jnp.sum(m, axis=0, keepdims=True)
    col = jnp.sum(m, axis=1, keepdims=True)
    a = (logit_scale * inv_x) * inv_r * d_log
    hi = a.astype(bf16)
    lo = (a - hi.astype(f32)).astype(bf16)
    term = dot(jnp.concatenate([hi, lo], axis=0), x, 1, 0)
    term = term[:64] + term[64:] - rt.astype(f32) * (inv_r * inv_r * col)
    return hi, lo, row, term


def kernel(
    x_hbm, go_hbm, rt_hbm, wu_hbm, wd_hbm, gx_hbm, gr_hbm, gu_hbm, gd_hbm,
    x_ref, go_ref, rt_ref, wu_ref, wd_ref,
    s1, r1, s2, r2, xg, parts, sibr, cs, rz, ry, fy, fz, s3, r3, s4, r4,
    tp, q1, t2, q2, t3, q3, t4, ro, act_ref, dpre_ref, gx, gr, gu, gd,
    lsem, ssem, rsem,
):
    loads = [
        pltpu.make_async_copy(a, b, lsem.at[i])
        for i, (a, b) in enumerate(
            [(x_hbm, x_ref), (rt_hbm, rt_ref), (go_hbm, go_ref), (wu_hbm, wu_ref), (wd_hbm, wd_ref)]
        )
    ]
    for c in loads:
        c.start()

    ex, dp = lax.axis_index("expert"), lax.axis_index("dp")
    G, M = ex // 2, (ex % 2) * 4 + dp
    kG, jG = k_of(G), j_of(G)

    def dev(g, m):
        return {"expert": 2 * g + m // 4, "dp": m % 4}

    group = [(G, (M + d) % N) for d in range(1, N)]
    outs = [(expert_of(M, j), (G + j) % N) for j in range(N)]
    ins = [((M - jG + N) % N + N * i, kG) for i in range(N)]
    far = [(G % N + N * ((G // N + d) % N), M) for d in range(1, N)]
    near = [((G // N) * N + (G % N + d) % N, M) for d in range(1, N)]

    def is_me(g, m):
        return jnp.logical_and(g == G, m == M)

    barrier = pltpu.get_barrier_semaphore()
    for g, m in group + far + near:
        pl.semaphore_signal(barrier, inc=1, device_id=dev(g, m), device_id_type=MESH)
    for g, m in outs + ins:

        @pl.when(jnp.logical_not(is_me(g, m)))
        def _():
            pl.semaphore_signal(barrier, inc=1, device_id=dev(g, m), device_id_type=MESH)

    mine = jnp.logical_and(kG == M, (G + jG) % N == M).astype(jnp.int32)

    sems = [0]
    pending = []

    def sems_of(n):
        at = sems[0]
        sems[0] += n
        return at

    def copy(src, dst, s, r, to):
        return pltpu.make_async_remote_copy(
            src_ref=src, dst_ref=dst, send_sem=ssem.at[s], recv_sem=rsem.at[r],
            device_id=dev(*to), device_id_type=MESH,
        )

    def all_to_all(src, dst):
        at = sems_of(N - 1)
        for d in range(1, N):
            to = (G, (M + d) % N)
            c = copy(src.at[to[1]], dst.at[M], at + d - 1, at + d - 1, to)
            c.start()
            pending.append((c, None))
        dst[M] = src[M]
        for d in range(1, N):
            came = (M - d + N) % N
            copy(src.at[came], dst.at[came], at + d - 1, at + d - 1, (G, came)).wait_recv()

    def exchange(src, dst, partners, slot, n):
        at = sems_of(n - 1)
        for d in range(1, n):
            c = copy(src, dst.at[slot], at + d - 1, at + d - 1, partners[d - 1])
            c.start()
            pending.append((c, None))
        dst[slot] = src[...]
        for d in range(1, n):
            came = (slot - d + n) % n
            copy(src, dst.at[came], at + d - 1, at + d - 1, partners[d - 1]).wait_recv()

    def cross(src, dst, to, slot, sources):
        at = sems_of(N)
        for b in range(N):
            c = copy(src.at[b], dst.at[slot], at + b, at + slot, to[b])
            me = is_me(*to[b])

            @pl.when(me)
            def _():
                dst[slot] = src[b]

            @pl.when(jnp.logical_not(me))
            def _():
                c.start()

            pending.append((c, me))
        for b in range(N):

            @pl.when(jnp.logical_not(is_me(*sources[b])))
            def _():
                copy(src.at[b], dst.at[b], at + b, at + b, sources[b]).wait_recv()

    def send(src, dst, to):
        at = sems_of(1)
        c = copy(src, dst, at, at, to)
        c.start()
        pending.append((c, None))
        return c

    for c in loads[:3]:
        c.wait()
    x, go, rt = x_ref[...], go_ref[...], rt_ref[...]
    *saved, slots, grads = front(x, go, rt)
    s1[...] = moved(by_member, jnp.concatenate([slots, grads], axis=0)).reshape(N, 16, D)
    pl.semaphore_wait(barrier, 7 * 3 + 16 - 2 * mine)

    all_to_all(s1, r1)
    s2[...] = moved(swapped, r1[...].reshape(128, D)).reshape(N, 16, D)
    cross(s2, r2, outs, G // N, ins)
    xg[M] = moved(halves_out, r2[...].reshape(128, D))

    my, mz = (M + 4) % N, M + 2 - 4 * ((M // 2) % 2)
    md = (mz + 4) % N

    def sib(m):
        return m + 1 - 2 * (m % 2)

    Y, Z, S = (G, my), (G, mz), (G, sib(M))
    top, low = pl.ds(0, 64), pl.ds(64, 64)
    own_y = send(xg.at[M], xg.at[M], Y)
    own_z = send(xg.at[M], xg.at[M], Z)
    own_s = send(xg.at[M], xg.at[M], S)
    own_y.wait_recv()
    ty = send(xg.at[my, top], xg.at[my, top], Z)
    sy = send(xg.at[my], xg.at[my], S)
    own_z.wait_recv()
    tz = send(xg.at[mz, low], xg.at[mz, low], Y)
    sz = send(xg.at[mz], xg.at[mz], S)
    ty.wait_recv()
    sd = send(xg.at[md, top], xg.at[md, top], S)
    tz.wait_recv()
    se = send(xg.at[md, low], xg.at[md, low], S)
    for c in (own_s, sy, sz, sd, se):
        c.wait_recv()

    loads[3].wait()
    loads[4].wait()

    @pl.loop(0, 4)
    def _(b):
        wu, wd = wu_ref[...], wd_ref[...]
        rows = xg[pl.ds(2 * b, 2), 0:64, :].reshape(128, D)
        grows = xg[pl.ds(2 * b, 2), 64:128, :].reshape(128, D)
        pre = dot(rows, wu, 1, 0)
        cdf = 0.5 * (1.0 + lax.erf(pre * 0.7071067811865476))
        pdf = 0.3989422804014327 * jnp.exp(-0.5 * pre * pre)
        act = (pre * cdf).astype(bf16)
        dpre = (dot(grows, wd, 1, 0) * (cdf + pre * pdf)).astype(bf16)
        at = pl.ds(pl.multiple_of(b * 128, 128), 128)
        act_ref[at, :] = act
        dpre_ref[at, :] = dpre
        parts[pl.ds(2 * b, 2), 0:64, :] = dot(act, wd, 1, 1).astype(bf16).reshape(2, 64, D)
        parts[pl.ds(2 * b, 2), 64:128, :] = dot(dpre, wu, 1, 1).astype(bf16).reshape(2, 64, D)

    order = (M, my, mz, md)
    to_sib = {q: send(parts.at[sib(order[q])], sibr.at[q], S) for q in (3, 1, 2, 0)}

    def chip_sum(q):
        to_sib[q].wait_recv()
        return parts[order[q]].astype(f32) + sibr[q].astype(f32)

    cs[3] = chip_sum(3).astype(bf16)
    dz = send(cs.at[3, top], rz, Z)
    dy = send(cs.at[3, low], ry, Y)
    v = chip_sum(1)
    dz.wait_recv()
    cs[1, 0:64, :] = (v[0:64] + rz[...].astype(f32)).astype(bf16)
    cs[1, 64:128, :] = v[64:128].astype(bf16)
    to_y = send(cs.at[1], fy, Y)
    v = chip_sum(2)
    dy.wait_recv()
    cs[2, 0:64, :] = v[0:64].astype(bf16)
    cs[2, 64:128, :] = (v[64:128] + ry[...].astype(f32)).astype(bf16)
    to_z = send(cs.at[2], fz, Z)

    grows = xg[:, 64:128, :].reshape(512, D)
    gd[...] = dot(grows, act_ref[...], 0, 0).astype(bf16)
    rows = xg[:, 0:64, :].reshape(512, D)
    gu[...] = dot(rows, dpre_ref[...], 0, 0).astype(bf16)
    stores = [
        pltpu.make_async_copy(gu, gu_hbm, lsem.at[5]),
        pltpu.make_async_copy(gd, gd_hbm, lsem.at[6]),
    ]
    for c in stores:
        c.start()

    v = chip_sum(0)
    to_y.wait_recv()
    to_z.wait_recv()
    total = (v + fy[...].astype(f32) + fz[...].astype(f32)).astype(bf16)

    s3[...] = moved(halves_in, total).reshape(N, 16, D)
    cross(s3, r3, ins, jG, outs)
    s4[...] = moved(swapped, r3[...].reshape(128, D)).reshape(N, 16, D)
    all_to_all(s4, r4)
    got = moved(by_expert, r4[...].reshape(128, D))
    slots_out, grad_slots = got[:64], got[64:]
    x, go, rt = x_ref[...], go_ref[...], rt_ref[...]
    hi, lo, row, term = back(x, go, rt, saved, slots_out, grad_slots)

    tb = term.astype(bf16)
    for m in range(N):
        r, zl = (m // 4) * 2 + m % 2, (m // 2) % 2
        tp[m] = tb[16 * r : 16 * r + 16, HALF_D * zl : HALF_D * (zl + 1)]
    all_to_all(tp, q1)

    left = jnp.concatenate([saved[3].astype(bf16), hi, lo], axis=0)
    right = jnp.concatenate([grad_slots, rt, rt], axis=0)
    inv_x = saved[0]
    gx[...] = (dot(left, right, 0, 0) - x.astype(f32) * to_column(inv_x * inv_x * row)).astype(bf16)
    out_x = pltpu.make_async_copy(gx, gx_hbm, lsem.at[7])
    out_x.start()
    stores.append(out_x)

    t2[...] = jnp.sum(q1[...].astype(f32), axis=0).astype(bf16)
    exchange(t2, q2, far, G // N, N)
    t3[...] = jnp.sum(q2[...].astype(f32), axis=0).astype(bf16)
    exchange(t3, q3, near, G % N, N)
    t4[...] = jnp.sum(q3[...].astype(f32), axis=0).astype(bf16)
    r, zl = (M // 4) * 2 + M % 2, (M // 2) % 2
    same = [(r + d) % 4 for d in range(1, 4)]
    exchange(t4, ro, [(G, (a // 2) * 4 + zl * 2 + a % 2) for a in same], r, 4)
    whole = ro[...].reshape(64, HALF_D).astype(f32)
    gr[...] = jnp.where(M % 2 == 0, whole[:, :320], whole[:, 320:])
    out_r = pltpu.make_async_copy(gr, gr_hbm, lsem.at[8])
    out_r.start()
    stores.append(out_r)

    for c, me in pending:
        if me is None:
            c.wait_send()
        else:
            pl.when(jnp.logical_not(me))(c.wait_send)
    for c in stores:
        c.wait()


N_SEMS = 7 + 8 + 9 + 8 + 8 + 7 + 7 + 7 + 7 + 3


def local(tokens, grad_out, router, up_weight, down_weight):
    block = pltpu.VMEM((N, 16, D), bf16)
    big = pltpu.VMEM((N, 128, D), bf16)
    piece = pltpu.VMEM((N, 16, HALF_D), bf16)
    one = pltpu.VMEM((16, HALF_D), bf16)
    weight = pltpu.VMEM((D, K), bf16)
    image = pltpu.VMEM((128, D), bf16)
    scratch = [
        image, image, pltpu.VMEM((64, D), bf16), weight, weight,
        block, block, block, block, big, big,
        pltpu.VMEM((4, 128, D), bf16), pltpu.VMEM((4, 128, D), bf16),
        pltpu.VMEM((64, D), bf16), pltpu.VMEM((64, D), bf16), image, image,
        block, block, block, block,
        piece, piece, one, piece, one, piece, one, pltpu.VMEM((4, 16, HALF_D), bf16),
        pltpu.VMEM((512, K), bf16), pltpu.VMEM((512, K), bf16),
        image, pltpu.VMEM((64, 320), f32), weight, weight,
        pltpu.SemaphoreType.DMA((9,)),
        pltpu.SemaphoreType.DMA((N_SEMS,)),
        pltpu.SemaphoreType.DMA((N_SEMS,)),
    ]
    anywhere = pl.BlockSpec(memory_space=pl.ANY)
    gx, gr, gu, gd = pl.pallas_call(
        kernel,
        out_shape=(
            jax.ShapeDtypeStruct((128, D), bf16),
            jax.ShapeDtypeStruct((64, 320), f32),
            jax.ShapeDtypeStruct((D, K), bf16),
            jax.ShapeDtypeStruct((D, K), bf16),
        ),
        in_specs=[anywhere] * 5,
        out_specs=(anywhere,) * 4,
        scratch_shapes=scratch,
        compiler_params=pltpu.CompilerParams(
            collective_id=0, has_side_effects=True, vmem_limit_bytes=56 * 2**20
        ),
        cost_estimate=pl.CostEstimate(flops=4 * 10**9, bytes_accessed=6 * 10**6, transcendentals=500000),
    )(tokens[0], grad_out[0], router.T, up_weight[0], down_weight[0])
    return (gx[None], gr.T, gu[None], gd[None])


def solution(mesh):
    placed = (
        P(("expert", "dp"), None, None),
        P(("expert", "dp"), None, None),
        P(),
        P("expert", None, "dp"),
        P("expert", None, "dp"),
    )
    return jax.shard_map(
        local,
        mesh=mesh,
        in_specs=placed,
        out_specs=(
            P(("expert", "dp"), None, None),
            P("dp", None),
            P("expert", None, "dp"),
            P("expert", None, "dp"),
        ),
        check_vma=False,
    )
```

```python
import functools

import jax
import jax.numpy as jnp
from jax import lax
from jax.experimental import pallas as pl
from jax.experimental.pallas import tpu as pltpu
from jax.sharding import PartitionSpec as P

logit_scale = 24.0
f32 = jnp.float32
bf16 = jnp.bfloat16
MESH = pl.DeviceIdType.MESH
N = 8
D = 1280
K = 384
HALF_D = 640


def dot(a, b, ca, cb):
    return lax.dot_general(a, b, (((ca,), (cb,)), ((), ())), preferred_element_type=f32)


def bits(m):
    return m // 4, (m // 2) % 2, m % 2


def flip(bit, by):
    return 1 - bit if by else bit


def step(g, dz, dx, dy):
    z, x, y = g // 16, (g // 4) % 4, g % 4
    return ((z + dz) % 4) * 16 + ((x + dx) % 4) * 4 + (y + dy) % 4


def receiver(g, m, j):
    yl, zl, c = bits(m)
    b, odd, dx1 = j // 4, 1 - (j // 2) % 2, j % 2
    dx0 = c * b + (1 - c) * flip(yl, b)
    dy = c * (3 - 2 * yl) + (1 - c) * 2 * b
    dz = 3 - 2 * zl if odd else 2 * flip(zl, dx1)
    to_y = c * (1 - yl) + (1 - c) * flip(yl, b)
    to_z = 1 - zl if odd else dx1
    i = b * 4 + (1 - odd) * 2 + flip(zl, dx1)
    return step(g, dz, dx1 * 2 + dx0, dy), to_y * 4 + to_z * 2 + c, i


def sender(e, t, i):
    yl, zl, c = bits(t)
    b, odd, q = i // 4, 1 - (i // 2) % 2, i % 2
    dx1 = flip(1 - zl, q) if odd else zl
    dz = 1 + 2 * zl if odd else 2 * q
    dy = c * (1 + 2 * yl) + (1 - c) * 2 * b
    dx0 = c * b + (1 - c) * yl
    from_y = c * (1 - yl) + (1 - c) * flip(yl, b)
    from_z = 1 - zl if odd else flip(zl, q)
    j = b * 4 + (1 - odd) * 2 + dx1
    return step(e, 4 - dz, 4 - (dx1 * 2 + dx0), 4 - dy), from_y * 4 + from_z * 2 + c, j


SELF = 2


def by_expert(g):
    def source(o):
        h, e = o >> 6, o & 63
        dz = ((e >> 4) - g // 16) & 3
        dx = ((e >> 2) - g // 4) & 3
        dy = (e - g) & 3
        dx0, dx1, c, odd = dx & 1, dx >> 1, dy & 1, dz & 1
        yl = c * (1 - (dy >> 1)) + (1 - c) * ((dy >> 1) ^ dx0)
        zl = odd * (1 - (dz >> 1)) + (1 - odd) * ((dz >> 1) ^ dx1)
        b = c * dx0 + (1 - c) * (dy >> 1)
        j = b * 4 + (1 - odd) * 2 + dx1
        return (yl * 4 + zl * 2 + c) * 16 + h * 8 + j

    return source


def pick(source, inverse=False):
    rows = lax.broadcasted_iota(jnp.int32, (128, 128), 0)
    cols = lax.broadcasted_iota(jnp.int32, (128, 128), 1)
    hit = rows == source(cols) if inverse else source(rows) == cols
    return jnp.where(hit, 1.0, 0.0).astype(bf16)


def swapped(o):
    return (o & 7) * 16 + ((o >> 3) & 1) * 8 + (o >> 4)


def moved(source, value, inverse=False):
    return dot(pick(source, inverse), value, 1, 0).astype(bf16)


def to_row(column):
    return jnp.broadcast_to(column, (128, 128)).T[0:1, :]


def to_column(row):
    return jnp.broadcast_to(row, (128, 128)).T[:, 0:1]


def front(x, go, rt):
    xf = x.astype(f32)
    rf = rt.astype(f32)
    inv_x = to_row(lax.rsqrt(jnp.sum(xf * xf, axis=1, keepdims=True) + 1e-06))
    inv_r = lax.rsqrt(jnp.sum(rf * rf, axis=1, keepdims=True) + 1e-06)
    logits = (logit_scale * inv_x) * inv_r * dot(rt, x, 1, 1)
    e = jnp.exp(logits)
    disp = e / jnp.sum(e, axis=1, keepdims=True)
    comb = e / jnp.sum(e, axis=0, keepdims=True)
    slots = dot(disp.astype(bf16), x, 1, 0).astype(bf16)
    grads = dot(comb.astype(bf16), go, 1, 0).astype(bf16)
    return inv_x, inv_r, logits, disp, comb, slots, grads


def back(x, go, rt, saved, slots_out, grad_slots):
    inv_x, inv_r, logits, disp, comb = saved
    d_comb = dot(slots_out, go, 1, 1).astype(bf16).astype(f32)
    d_disp = dot(grad_slots, x, 1, 1).astype(bf16).astype(f32)
    d_log = disp * (d_disp - jnp.sum(disp * d_disp, axis=1, keepdims=True)) + comb * (
        d_comb - jnp.sum(comb * d_comb, axis=0, keepdims=True)
    )
    m = d_log * logits
    row = jnp.sum(m, axis=0, keepdims=True)
    col = jnp.sum(m, axis=1, keepdims=True)
    a = (logit_scale * inv_x) * inv_r * d_log
    hi = a.astype(bf16)
    lo = (a - hi.astype(f32)).astype(bf16)
    term = dot(jnp.concatenate([hi, lo], axis=0), x, 1, 0)
    term = term[:64] + term[64:] - rt.astype(f32) * (inv_r * inv_r * col)
    return hi, lo, row, term


def kernel(
    x_hbm, go_hbm, rt_hbm, wu_hbm, wd_hbm, gx_hbm, gr_hbm, gu_hbm, gd_hbm,
    x_ref, go_ref, rt_ref, wu_ref, wd_ref,
    s1, r1, s2, xg, xs, gs, parts, sibr, cs, rel, fy, fz, s3, r3, s4, r4,
    tp, q1, t2, q2, t3, q3, t4, ro, act_ref, dpre_ref, gx, gr, gu, gd,
    lsem, ssem, rsem,
):
    loads = [
        pltpu.make_async_copy(a, b, lsem.at[i])
        for i, (a, b) in enumerate(
            [(x_hbm, x_ref), (rt_hbm, rt_ref), (go_hbm, go_ref), (wu_hbm, wu_ref), (wd_hbm, wd_ref)]
        )
    ]
    for c in loads:
        c.start()

    ex, dp = lax.axis_index("expert"), lax.axis_index("dp")
    G, M = ex // 2, (ex % 2) * 4 + dp

    def dev(g, m):
        return {"expert": 2 * g + m // 4, "dp": m % 4}

    group = [(G, (M + d) % N) for d in range(1, N)]
    outs = [receiver(G, M, j) for j in range(N)]
    ins = [sender(G, M, i) for i in range(N)]
    far = [(G % N + N * ((G // N + d) % N), M) for d in range(1, N)]
    near = [((G // N) * N + (G % N + d) % N, M) for d in range(1, N)]
    keeps = M == 0

    barrier = pltpu.get_barrier_semaphore()

    def greet(g, m):
        pl.semaphore_signal(barrier, inc=1, device_id=dev(g, m), device_id_type=MESH)

    for g, m in group + far + near:
        greet(g, m)
    for n in range(N):
        for g, m, _ in (outs[n], ins[n]):
            if n == SELF:
                pl.when(jnp.logical_not(keeps))(functools.partial(greet, g, m))
            else:
                greet(g, m)

    sems = [0]
    pending = []

    def sems_of(n):
        at = sems[0]
        sems[0] += n
        return at

    def copy(src, dst, s, r, to):
        return pltpu.make_async_remote_copy(
            src_ref=src, dst_ref=dst, send_sem=ssem.at[s], recv_sem=rsem.at[r],
            device_id=dev(*to), device_id_type=MESH,
        )

    def all_to_all(src, dst):
        at = sems_of(N - 1)
        for d in range(1, N):
            to = (G, (M + d) % N)
            c = copy(src.at[to[1]], dst.at[M], at + d - 1, at + d - 1, to)
            c.start()
            pending.append((c, None))
        dst[M] = src[M]

        def wait():
            for d in range(1, N):
                came = (M - d + N) % N
                copy(src.at[came], dst.at[came], at + d - 1, at + d - 1, (G, came)).wait_recv()

        return wait

    def exchange(src, dst, partners, slot, n):
        at = sems_of(n - 1)
        for d in range(1, n):
            c = copy(src, dst.at[slot], at + d - 1, at + d - 1, partners[d - 1])
            c.start()
            pending.append((c, None))
        dst[slot] = src[...]
        for d in range(1, n):
            came = (slot - d + n) % n
            copy(src, dst.at[came], at + d - 1, at + d - 1, partners[d - 1]).wait_recv()

    def unless(me, do):
        if me is None:
            do()
        else:
            pl.when(jnp.logical_not(me))(do)

    def cross_send(at, n, src, dst, own, to):
        c = copy(src, dst, at + n, at + to[2], to[:2])
        me = keeps if n == SELF else None
        unless(me, c.start)
        if me is not None:

            @pl.when(me)
            def _():
                own[...] = src[...]

        pending.append((c, me))

    def cross_wait(at, n, dst, source):
        unless(keeps if n == SELF else None, copy(dst, dst, at + n, at + n, source[:2]).wait_recv)

    def send(src, dst, to):
        at = sems_of(1)
        c = copy(src, dst, at, at, to)
        c.start()
        pending.append((c, None))
        return c

    for c in loads[:3]:
        c.wait()
    x, go, rt = x_ref[...], go_ref[...], rt_ref[...]
    *saved, slots, grads = front(x, go, rt)
    slotted = jnp.concatenate([slots, grads], axis=0)
    s1[...] = moved(by_expert(G), slotted, inverse=True).reshape(N, 16, D)
    pl.semaphore_wait(barrier, 7 * 3 + 16 - 2 * (1 - jnp.minimum(M, 1)))

    all_to_all(s1, r1)()
    s2[...] = moved(swapped, r1[...].reshape(128, D)).reshape(N, 16, D)
    at2, at3 = sems_of(N), sems_of(N)
    for j in range(N):
        g, t, i = outs[j]
        cross_send(at2, j, s2.at[j], xg.at[t, i], xg.at[M, SELF], outs[j])

    yl, zl, c0 = bits(M)
    my, mz, md = M + 4 - 8 * yl, M + 2 - 4 * zl, 7 - M + 2 * c0 - 1
    ms = 1 - 2 * c0
    chip, chip_y, chip_z, chip_d = M // 2, my // 2, mz // 2, md // 2
    Y, Z, S = (G, my), (G, mz), (G, M + ms)
    marks = {}

    def rows_of(m, q):
        return xg.at[m, pl.ds(2 * q, 2)]

    def spread(m, q, name, to):
        marks[name, q] = send(rows_of(m, q), rows_of(m, q), to)

    def stage_a(q):
        for i in (2 * q, 2 * q + 1):
            cross_wait(at2, i, xg.at[M, i], ins[i])
        spread(M, q, "y", Y)
        spread(M, q, "z", Z)
        spread(M, q, "s", S)

    def stage_b(q):
        marks["y", q].wait_recv()
        if q < 2:
            spread(my, q, "d", Z)
        spread(my, q, "sy", S)
        marks["z", q].wait_recv()
        if q >= 2:
            spread(mz, q, "d", Y)
        spread(mz, q, "sz", S)

    def stage_c(q):
        marks["d", q].wait_recv()
        spread(md, q, "sd", S)

    def stage_d(q):
        for name in ("s", "sy", "sz", "sd"):
            marks[name, q].wait_recv()
        if q == 0:
            loads[3].wait()
            loads[4].wait()
        wu, wd = wu_ref[...], wd_ref[...]
        both = xg[:, 2 * q : 2 * q + 2].astype(f32).reshape(16, 2, 8, D)
        rows = both[:, 0].reshape(128, D).astype(bf16)
        grows = both[:, 1].reshape(128, D).astype(bf16)
        at = slice(128 * q, 128 * q + 128)
        xs[at, :] = rows
        gs[at, :] = grows
        pre = dot(rows, wu, 1, 0)
        cdf = 0.5 * (1.0 + lax.erf(pre * 0.7071067811865476))
        pdf = 0.3989422804014327 * jnp.exp(-0.5 * pre * pre)
        act = (pre * cdf).astype(bf16)
        dpre = (dot(grows, wd, 1, 0) * (cdf + pre * pdf)).astype(bf16)
        act_ref[at, :] = act
        dpre_ref[at, :] = dpre
        out = dot(act, wd, 1, 1).reshape(16, 1, 8, D)
        back_out = dot(dpre, wu, 1, 1).reshape(16, 1, 8, D)
        mixed = jnp.concatenate([out, back_out], axis=1).reshape(16, 16, D).astype(bf16)
        parts[q] = mixed.reshape(4, 2, 2, 16, D)
        marks["p", q] = send(parts.at[q, :, 1 - c0], sibr.at[q], S)

    def chip_sum(q, to):
        return parts[q, to, c0].astype(f32) + sibr[q, to].astype(f32)

    def forward(q, n, value, dst, name, to):
        cs[q, n] = value.astype(bf16)
        marks[name, q] = send(cs.at[q, n], dst.at[q], to)

    def stage_e(q):
        marks["p", q].wait_recv()
        diagonal = chip_sum(q, chip_d)
        if q < 2:
            forward(q, 0, diagonal, rel, "r", Z)
            forward(q, 1, chip_sum(q, chip_z), fz, "fz", Z)
        else:
            forward(q, 0, diagonal, rel, "r", Y)
            forward(q, 1, chip_sum(q, chip_y), fy, "fy", Y)

    def stage_f(q):
        marks["r", q].wait_recv()
        if q < 2:
            forward(q, 2, chip_sum(q, chip_y) + rel[q].astype(f32), fy, "fy", Y)
        else:
            forward(q, 2, chip_sum(q, chip_z) + rel[q].astype(f32), fz, "fz", Z)

    def stage_g(q):
        marks["fy", q].wait_recv()
        marks["fz", q].wait_recv()
        total = chip_sum(q, chip) + fy[q].astype(f32) + fz[q].astype(f32)
        s3[2 * q : 2 * q + 2] = total.astype(bf16)
        for i in (2 * q, 2 * q + 1):
            g, t, j = ins[i]
            cross_send(at3, i, s3.at[i], r3.at[j], r3.at[SELF], ins[i])

    chain = ((stage_a, 0), (stage_b, 1), (stage_c, 2), (stage_e, 4), (stage_f, 5), (stage_g, 6), (stage_d, 3))
    for t in range(4 + 6):
        for run, late in chain:
            if 0 <= t - late < 4:
                run(t - late)

    gd[...] = dot(gs[...], act_ref[...], 0, 0).astype(bf16)
    stores = [pltpu.make_async_copy(gd, gd_hbm, lsem.at[6])]
    stores[0].start()

    for j in range(N):
        cross_wait(at3, j, r3.at[j], outs[j])
    s4[...] = moved(swapped, r3[...].reshape(128, D)).reshape(N, 16, D)
    wait = all_to_all(s4, r4)
    gu[...] = dot(xs[...], dpre_ref[...], 0, 0).astype(bf16)
    stores.append(pltpu.make_async_copy(gu, gu_hbm, lsem.at[5]))
    stores[1].start()
    wait()
    got = moved(by_expert(G), r4[...].reshape(128, D))
    slots_out, grad_slots = got[:64], got[64:]
    x, go, rt = x_ref[...], go_ref[...], rt_ref[...]
    hi, lo, row, term = back(x, go, rt, saved, slots_out, grad_slots)

    tb = term.astype(bf16)
    for m in range(N):
        r, zh = (m // 4) * 2 + m % 2, (m // 2) % 2
        tp[m] = tb[16 * r : 16 * r + 16, HALF_D * zh : HALF_D * (zh + 1)]
    wait = all_to_all(tp, q1)

    left = jnp.concatenate([saved[3].astype(bf16), hi, lo], axis=0)
    right = jnp.concatenate([grad_slots, rt, rt], axis=0)
    inv_x = saved[0]
    gx[...] = (dot(left, right, 0, 0) - x.astype(f32) * to_column(inv_x * inv_x * row)).astype(bf16)
    stores.append(pltpu.make_async_copy(gx, gx_hbm, lsem.at[7]))
    stores[2].start()
    wait()
    t2[...] = jnp.sum(q1[...].astype(f32), axis=0).astype(bf16)
    exchange(t2, q2, far, G // N, N)
    t3[...] = jnp.sum(q2[...].astype(f32), axis=0).astype(bf16)
    exchange(t3, q3, near, G % N, N)
    t4[...] = jnp.sum(q3[...].astype(f32), axis=0).astype(bf16)
    r = yl * 2 + c0
    same = [(r + d) % 4 for d in range(1, 4)]
    exchange(t4, ro, [(G, (a // 2) * 4 + zl * 2 + a % 2) for a in same], r, 4)
    whole = ro[...].reshape(64, HALF_D).astype(f32)
    gr[...] = jnp.where(c0 == 0, whole[:, :320], whole[:, 320:])
    stores.append(pltpu.make_async_copy(gr, gr_hbm, lsem.at[8]))
    stores[3].start()

    for c, me in pending:
        unless(me, c.wait_send)
    for c in stores:
        c.wait()


def keep(*refs):
    ins, outs, bufs, sem = refs[:4], refs[4:8], refs[8:12], refs[12]
    parts = [(n, h) for n in (2, 3, 0, 1) for h in (0, 1)]

    def part(ref, h):
        half = ref.shape[0] // 2
        return ref.at[pl.ds(h * half, half)]

    reads = [
        pltpu.make_async_copy(part(ins[n], h), part(bufs[n], h), sem.at[0, n, h]) for n, h in parts
    ]
    writes = [
        pltpu.make_async_copy(part(bufs[n], h), part(outs[n], h), sem.at[1, n, h]) for n, h in parts
    ]
    for one in reads:
        one.start()
    for one, two in zip(reads, writes):
        one.wait()
        two.start()
    for two in writes:
        two.wait()


N_SEMS = 7 + 8 + 8 + 4 * (7 + 4) + 7 + 7 + 7 + 7 + 3


def local(tokens, grad_out, router, up_weight, down_weight):
    block = pltpu.VMEM((N, 16, D), bf16)
    piece = pltpu.VMEM((N, 16, HALF_D), bf16)
    one = pltpu.VMEM((16, HALF_D), bf16)
    weight = pltpu.VMEM((D, K), bf16)
    image = pltpu.VMEM((128, D), bf16)
    four = pltpu.VMEM((4, 2, 16, D), bf16)
    scratch = [
        image, image, pltpu.VMEM((64, D), bf16), weight, weight,
        block, block, block, pltpu.VMEM((N, N, 16, D), bf16),
        pltpu.VMEM((512, D), bf16), pltpu.VMEM((512, D), bf16),
        pltpu.VMEM((4, 4, 2, 2, 16, D), bf16), pltpu.VMEM((4, 4, 2, 16, D), bf16),
        pltpu.VMEM((4, 3, 2, 16, D), bf16), four, four, four,
        block, block, block, block,
        piece, piece, one, piece, one, piece, one, pltpu.VMEM((4, 16, HALF_D), bf16),
        pltpu.VMEM((512, K), bf16), pltpu.VMEM((512, K), bf16),
        image, pltpu.VMEM((64, 320), f32), weight, weight,
        pltpu.SemaphoreType.DMA((9,)),
        pltpu.SemaphoreType.DMA((N_SEMS,)),
        pltpu.SemaphoreType.DMA((N_SEMS,)),
    ]
    anywhere = pl.BlockSpec(memory_space=pl.ANY)
    shapes = (
        jax.ShapeDtypeStruct((128, D), bf16),
        jax.ShapeDtypeStruct((64, 320), f32),
        jax.ShapeDtypeStruct((D, K), bf16),
        jax.ShapeDtypeStruct((D, K), bf16),
    )
    made = pl.pallas_call(
        kernel,
        out_shape=shapes,
        in_specs=[anywhere] * 5,
        out_specs=(anywhere,) * 4,
        scratch_shapes=scratch,
        compiler_params=pltpu.CompilerParams(
            collective_id=0, has_side_effects=True, vmem_limit_bytes=56 * 2**20
        ),
        cost_estimate=pl.CostEstimate(flops=4 * 10**9, bytes_accessed=6 * 10**6, transcendentals=500000),
    )(tokens[0], grad_out[0], router.T, up_weight[0], down_weight[0])
    gx, gr, gu, gd = pl.pallas_call(
        keep,
        out_shape=shapes,
        in_specs=[anywhere] * 4,
        out_specs=(anywhere,) * 4,
        scratch_shapes=[
            image, pltpu.VMEM((64, 320), f32), weight, weight, pltpu.SemaphoreType.DMA((2, 4, 2))
        ],
        compiler_params=pltpu.CompilerParams(vmem_limit_bytes=56 * 2**20),
    )(*made)
    return (gx[None], gr.T, gu[None], gd[None])


def solution(mesh):
    placed = (
        P(("expert", "dp"), None, None),
        P(("expert", "dp"), None, None),
        P(),
        P("expert", None, "dp"),
        P("expert", None, "dp"),
    )
    return jax.shard_map(
        local,
        mesh=mesh,
        in_specs=placed,
        out_specs=(
            P(("expert", "dp"), None, None),
            P("dp", None),
            P("expert", None, "dp"),
            P("expert", None, "dp"),
        ),
        check_vma=False,
    )
```

```python
import functools

import jax
import jax.numpy as jnp
from jax import lax
from jax.experimental import pallas as pl
from jax.experimental.pallas import tpu as pltpu
from jax.sharding import PartitionSpec as P

logit_scale = 24.0
f32 = jnp.float32
bf16 = jnp.bfloat16
MESH = pl.DeviceIdType.MESH
N = 8
D = 1280
K = 384
HALF_D = 640
ORDER = 'A3A2A1B3C3A0B2C2D3B1C1E3D2B0C0E2D1G3E1D0G2E0G1G0'


def dot(a, b, ca, cb):
    return lax.dot_general(a, b, (((ca,), (cb,)), ((), ())), preferred_element_type=f32)


def bits(m):
    return m // 4, (m // 2) % 2, m % 2


def flip(bit, by):
    return 1 - bit if by else bit


def step(g, dz, dx, dy):
    z, x, y = g // 16, (g // 4) % 4, g % 4
    return ((z + dz) % 4) * 16 + ((x + dx) % 4) * 4 + (y + dy) % 4


def receiver(g, m, j):
    yl, zl, c = bits(m)
    b, odd, dx1 = j // 4, 1 - (j // 2) % 2, j % 2
    dx0 = c * b + (1 - c) * flip(yl, b)
    dy = c * (3 - 2 * yl) + (1 - c) * 2 * b
    dz = 3 - 2 * zl if odd else 2 * flip(zl, dx1)
    to_y = c * (1 - yl) + (1 - c) * flip(yl, b)
    to_z = 1 - zl if odd else dx1
    i = b * 4 + (1 - odd) * 2 + flip(zl, dx1)
    return step(g, dz, dx1 * 2 + dx0, dy), to_y * 4 + to_z * 2 + c, i


def sender(e, t, i):
    yl, zl, c = bits(t)
    b, odd, q = i // 4, 1 - (i // 2) % 2, i % 2
    dx1 = flip(1 - zl, q) if odd else zl
    dz = 1 + 2 * zl if odd else 2 * q
    dy = c * (1 + 2 * yl) + (1 - c) * 2 * b
    dx0 = c * b + (1 - c) * yl
    from_y = c * (1 - yl) + (1 - c) * flip(yl, b)
    from_z = 1 - zl if odd else flip(zl, q)
    j = b * 4 + (1 - odd) * 2 + dx1
    return step(e, 4 - dz, 4 - (dx1 * 2 + dx0), 4 - dy), from_y * 4 + from_z * 2 + c, j


SELF = 2


def by_expert(g):
    def source(o):
        h, e = o >> 6, o & 63
        dz = ((e >> 4) - g // 16) & 3
        dx = ((e >> 2) - g // 4) & 3
        dy = (e - g) & 3
        dx0, dx1, c, odd = dx & 1, dx >> 1, dy & 1, dz & 1
        yl = c * (1 - (dy >> 1)) + (1 - c) * ((dy >> 1) ^ dx0)
        zl = odd * (1 - (dz >> 1)) + (1 - odd) * ((dz >> 1) ^ dx1)
        b = c * dx0 + (1 - c) * (dy >> 1)
        j = b * 4 + (1 - odd) * 2 + dx1
        return (yl * 4 + zl * 2 + c) * 16 + h * 8 + j

    return source


def pick(source, inverse=False):
    rows = lax.broadcasted_iota(jnp.int32, (128, 128), 0)
    cols = lax.broadcasted_iota(jnp.int32, (128, 128), 1)
    hit = rows == source(cols) if inverse else source(rows) == cols
    return jnp.where(hit, 1.0, 0.0).astype(bf16)


def swapped(o):
    return (o & 7) * 16 + ((o >> 3) & 1) * 8 + (o >> 4)


def moved(source, value, inverse=False):
    return dot(pick(source, inverse), value, 1, 0).astype(bf16)


def to_row(column):
    return jnp.broadcast_to(column, (128, 128)).T[0:1, :]


def to_column(row):
    return jnp.broadcast_to(row, (128, 128)).T[:, 0:1]


def front(x, go, rt):
    xf = x.astype(f32)
    rf = rt.astype(f32)
    inv_x = to_row(lax.rsqrt(jnp.sum(xf * xf, axis=1, keepdims=True) + 1e-06))
    inv_r = lax.rsqrt(jnp.sum(rf * rf, axis=1, keepdims=True) + 1e-06)
    logits = (logit_scale * inv_x) * inv_r * dot(rt, x, 1, 1)
    e = jnp.exp(logits)
    disp = e / jnp.sum(e, axis=1, keepdims=True)
    comb = e / jnp.sum(e, axis=0, keepdims=True)
    slots = dot(disp.astype(bf16), x, 1, 0).astype(bf16)
    grads = dot(comb.astype(bf16), go, 1, 0).astype(bf16)
    return inv_x, inv_r, logits, disp, comb, slots, grads


def back(x, go, rt, saved, slots_out, grad_slots):
    inv_x, inv_r, logits, disp, comb = saved
    d_comb = dot(slots_out, go, 1, 1).astype(bf16).astype(f32)
    d_disp = dot(grad_slots, x, 1, 1).astype(bf16).astype(f32)
    d_log = disp * (d_disp - jnp.sum(disp * d_disp, axis=1, keepdims=True)) + comb * (
        d_comb - jnp.sum(comb * d_comb, axis=0, keepdims=True)
    )
    m = d_log * logits
    row = jnp.sum(m, axis=0, keepdims=True)
    col = jnp.sum(m, axis=1, keepdims=True)
    a = (logit_scale * inv_x) * inv_r * d_log
    hi = a.astype(bf16)
    lo = (a - hi.astype(f32)).astype(bf16)
    term = dot(jnp.concatenate([hi, lo], axis=0), x, 1, 0)
    term = term[:64] + term[64:] - rt.astype(f32) * (inv_r * inv_r * col)
    return hi, lo, row, term


def kernel(
    x_hbm, go_hbm, rt_hbm, wu_hbm, wd_hbm, gx_hbm, gr_hbm, gu_hbm, gd_hbm,
    x_ref, go_ref, rt_ref, wu_ref, wd_ref,
    s1, r1, s2, xg, xs, gs, parts, sibr, cs, rel, fy, fz, s3, r3, s4, r4,
    tp, q1, t2, q2, t3, q3, t4, ro, act_ref, dpre_ref, gx, gr, gu, gd,
    lsem, ssem, rsem,
):
    loads = [
        pltpu.make_async_copy(a, b, lsem.at[i])
        for i, (a, b) in enumerate(
            [(x_hbm, x_ref), (rt_hbm, rt_ref), (go_hbm, go_ref), (wu_hbm, wu_ref), (wd_hbm, wd_ref)]
        )
    ]
    for c in loads[:3]:
        c.start()

    ex, dp = lax.axis_index("expert"), lax.axis_index("dp")
    G, M = ex // 2, (ex % 2) * 4 + dp

    def dev(g, m):
        return {"expert": 2 * g + m // 4, "dp": m % 4}

    group = [(G, (M + d) % N) for d in range(1, N)]
    outs = [receiver(G, M, j) for j in range(N)]
    ins = [sender(G, M, i) for i in range(N)]
    far = [(G % N + N * ((G // N + d) % N), M) for d in range(1, N)]
    near = [((G // N) * N + (G % N + d) % N, M) for d in range(1, N)]
    keeps = M == 0

    barrier = pltpu.get_barrier_semaphore()

    def greet(g, m):
        pl.semaphore_signal(barrier, inc=1, device_id=dev(g, m), device_id_type=MESH)

    for g, m in group + far + near:
        greet(g, m)
    for n in range(N):
        for g, m, _ in (outs[n], ins[n]):
            if n == SELF:
                pl.when(jnp.logical_not(keeps))(functools.partial(greet, g, m))
            else:
                greet(g, m)

    sems = [0]
    pending = []

    def sems_of(n):
        at = sems[0]
        sems[0] += n
        return at

    def copy(src, dst, s, r, to):
        return pltpu.make_async_remote_copy(
            src_ref=src, dst_ref=dst, send_sem=ssem.at[s], recv_sem=rsem.at[r],
            device_id=dev(*to), device_id_type=MESH,
        )

    def all_to_all(src, dst):
        at = sems_of(N - 1)
        for d in range(1, N):
            to = (G, (M + d) % N)
            c = copy(src.at[to[1]], dst.at[M], at + d - 1, at + d - 1, to)
            c.start()
            pending.append((c, None))
        dst[M] = src[M]

        def wait():
            for d in range(1, N):
                came = (M - d + N) % N
                copy(src.at[came], dst.at[came], at + d - 1, at + d - 1, (G, came)).wait_recv()

        return wait

    def exchange(src, dst, partners, slot, n):
        at = sems_of(n - 1)
        for d in range(1, n):
            c = copy(src, dst.at[slot], at + d - 1, at + d - 1, partners[d - 1])
            c.start()
            pending.append((c, None))
        dst[slot] = src[...]
        drain(n - 1)
        for d in range(1, n):
            came = (slot - d + n) % n
            copy(src, dst.at[came], at + d - 1, at + d - 1, partners[d - 1]).wait_recv()

    def unless(me, do):
        if me is None:
            do()
        else:
            pl.when(jnp.logical_not(me))(do)

    def cross_send(at, n, src, dst, own, to):
        c = copy(src, dst, at + n, at + to[2], to[:2])
        me = keeps if n == SELF else None
        unless(me, c.start)
        if me is not None:

            @pl.when(me)
            def _():
                own[...] = src[...]

        pending.append((c, me))

    def cross_wait(at, n, dst, source):
        unless(keeps if n == SELF else None, copy(dst, dst, at + n, at + n, source[:2]).wait_recv)

    def drain(keep):
        while len(pending) > keep:
            c, me = pending.pop(0)
            unless(me, c.wait_send)

    def send(src, dst, to):
        at = sems_of(1)
        c = copy(src, dst, at, at, to)
        c.start()
        pending.append((c, None))
        return c

    for c in loads[:3]:
        c.wait()
    for c in loads[3:]:
        c.start()
    x, go, rt = x_ref[...], go_ref[...], rt_ref[...]
    *saved, slots, grads = front(x, go, rt)
    slotted = jnp.concatenate([slots, grads], axis=0)
    s1[...] = moved(by_expert(G), slotted, inverse=True).reshape(N, 16, D)
    pl.semaphore_wait(barrier, 7 * 3 + 16 - 2 * (1 - jnp.minimum(M, 1)))

    all_to_all(s1, r1)()
    s2[...] = moved(swapped, r1[...].reshape(128, D)).reshape(N, 16, D)
    at2, at3 = sems_of(N), sems_of(N)
    for j in (6, 7, 4, 5, 2, 3, 0, 1):
        g, t, i = outs[j]
        cross_send(at2, j, s2.at[j], xg.at[t, i], xg.at[M, SELF], outs[j])

    yl, zl, c0 = bits(M)
    my, mz, md = M + 4 - 8 * yl, M + 2 - 4 * zl, 7 - M + 2 * c0 - 1
    ms = 1 - 2 * c0
    chip, chip_y, chip_z, chip_d = M // 2, my // 2, mz // 2, md // 2
    Y, Z, S = (G, my), (G, mz), (G, M + ms)
    marks = {}

    def rows_of(m, q):
        return xg.at[m, pl.ds(2 * q, 2)]

    def spread(m, q, name, to):
        marks[name, q] = send(rows_of(m, q), rows_of(m, q), to)

    O = (G, md)

    def stage_a(q):
        for i in (2 * q, 2 * q + 1):
            cross_wait(at2, i, xg.at[M, i], ins[i])
        spread(M, q, "y", Y)
        spread(M, q, "z", Z)
        spread(M, q, "d", O)
        spread(M, q, "s", S)

    def stage_b(q):
        marks["y", q].wait_recv()
        spread(my, q, "sy", S)
        marks["z", q].wait_recv()
        spread(mz, q, "sz", S)

    def stage_c(q):
        marks["d", q].wait_recv()
        spread(md, q, "sd", S)

    def stage_d(q):
        for name in ("s", "sy", "sz", "sd"):
            marks[name, q].wait_recv()
        if str(q) == ORDER[ORDER.index("D") + 1]:
            loads[3].wait()
            loads[4].wait()
        wu, wd = wu_ref[...], wd_ref[...]
        both = xg[:, 2 * q : 2 * q + 2].astype(f32).reshape(16, 2, 8, D)
        rows = both[:, 0].reshape(128, D).astype(bf16)
        grows = both[:, 1].reshape(128, D).astype(bf16)
        at = slice(128 * q, 128 * q + 128)
        xs[at, :] = rows
        gs[at, :] = grows
        pre = dot(rows, wu, 1, 0)
        cdf = 0.5 * (1.0 + lax.erf(pre * 0.7071067811865476))
        pdf = 0.3989422804014327 * jnp.exp(-0.5 * pre * pre)
        act = (pre * cdf).astype(bf16)
        dpre = (dot(grows, wd, 1, 0) * (cdf + pre * pdf)).astype(bf16)
        act_ref[at, :] = act
        dpre_ref[at, :] = dpre
        out = dot(act, wd, 1, 1).reshape(16, 1, 8, D)
        back_out = dot(dpre, wu, 1, 1).reshape(16, 1, 8, D)
        mixed = jnp.concatenate([out, back_out], axis=1).reshape(16, 16, D).astype(bf16)
        parts[q] = mixed.reshape(4, 2, 2, 16, D)
        marks["p", q] = send(parts.at[q, :, 1 - c0], sibr.at[q], S)

    def chip_sum(q, to):
        return parts[q, to, c0].astype(f32) + sibr[q, to].astype(f32)

    def forward(q, n, value, dst, name, to):
        cs[q, n] = value.astype(bf16)
        marks[name, q] = send(cs.at[q, n], dst.at[q], to)

    def stage_e(q):
        marks["p", q].wait_recv()
        forward(q, 0, chip_sum(q, chip_d), rel, "r", O)
        forward(q, 1, chip_sum(q, chip_z), fz, "fz", Z)
        forward(q, 2, chip_sum(q, chip_y), fy, "fy", Y)

    def stage_g(q):
        for name in ("fy", "fz", "r"):
            marks[name, q].wait_recv()
        total = chip_sum(q, chip) + fy[q].astype(f32) + fz[q].astype(f32) + rel[q].astype(f32)
        s3[2 * q : 2 * q + 2] = total.astype(bf16)
        for i in (2 * q + 1, 2 * q):
            g, t, j = ins[i]
            cross_send(at3, i, s3.at[i], r3.at[j], r3.at[SELF], ins[i])

    stages = {"A": stage_a, "B": stage_b, "C": stage_c, "D": stage_d, "E": stage_e, "G": stage_g}
    for n in range(len(ORDER) // 2):
        stages[ORDER[2 * n]](int(ORDER[2 * n + 1]))

    gd[...] = dot(gs[...], act_ref[...], 0, 0).astype(bf16)
    stores = [pltpu.make_async_copy(gd, gd_hbm, lsem.at[6])]
    stores[0].start()

    drain(8)

    for j in range(N):
        cross_wait(at3, j, r3.at[j], outs[j])
    s4[...] = moved(swapped, r3[...].reshape(128, D)).reshape(N, 16, D)
    wait = all_to_all(s4, r4)
    gu[...] = dot(xs[...], dpre_ref[...], 0, 0).astype(bf16)
    stores.append(pltpu.make_async_copy(gu, gu_hbm, lsem.at[5]))
    stores[1].start()
    drain(7)
    wait()
    got = moved(by_expert(G), r4[...].reshape(128, D))
    slots_out, grad_slots = got[:64], got[64:]
    x, go, rt = x_ref[...], go_ref[...], rt_ref[...]
    hi, lo, row, term = back(x, go, rt, saved, slots_out, grad_slots)

    tb = term.astype(bf16)
    for m in range(N):
        r, zh = (m // 4) * 2 + m % 2, (m // 2) % 2
        tp[m] = tb[16 * r : 16 * r + 16, HALF_D * zh : HALF_D * (zh + 1)]
    wait = all_to_all(tp, q1)

    left = jnp.concatenate([saved[3].astype(bf16), hi, lo], axis=0)
    right = jnp.concatenate([grad_slots, rt, rt], axis=0)
    inv_x = saved[0]
    gx[...] = (dot(left, right, 0, 0) - x.astype(f32) * to_column(inv_x * inv_x * row)).astype(bf16)
    stores.append(pltpu.make_async_copy(gx, gx_hbm, lsem.at[7]))
    stores[2].start()
    wait()
    t2[...] = jnp.sum(q1[...].astype(f32), axis=0).astype(bf16)
    exchange(t2, q2, far, G // N, N)
    t3[...] = jnp.sum(q2[...].astype(f32), axis=0).astype(bf16)
    exchange(t3, q3, near, G % N, N)
    t4[...] = jnp.sum(q3[...].astype(f32), axis=0).astype(bf16)
    r = yl * 2 + c0
    same = [(r + d) % 4 for d in range(1, 4)]
    exchange(t4, ro, [(G, (a // 2) * 4 + zl * 2 + a % 2) for a in same], r, 4)
    whole = ro[...].reshape(64, HALF_D).astype(f32)
    gr[...] = jnp.where(c0 == 0, whole[:, :320], whole[:, 320:])
    stores.append(pltpu.make_async_copy(gr, gr_hbm, lsem.at[8]))
    stores[3].start()

    drain(0)
    for c in stores:
        c.wait()


def keep(*refs):
    ins, outs, bufs, sem = refs[:4], refs[4:8], refs[8:12], refs[12]
    parts = [(n, h) for n in (2, 3, 0, 1) for h in (0, 1)]

    def part(ref, h):
        half = ref.shape[0] // 2
        return ref.at[pl.ds(h * half, half)]

    reads = [
        pltpu.make_async_copy(part(ins[n], h), part(bufs[n], h), sem.at[0, n, h]) for n, h in parts
    ]
    writes = [
        pltpu.make_async_copy(part(bufs[n], h), part(outs[n], h), sem.at[1, n, h]) for n, h in parts
    ]
    for one in reads:
        one.start()
    for one, two in zip(reads, writes):
        one.wait()
        two.start()
    for two in writes:
        two.wait()


N_SEMS = 7 + 8 + 8 + 4 * (7 + 4) + 7 + 7 + 7 + 7 + 3


def local(tokens, grad_out, router, up_weight, down_weight):
    block = pltpu.VMEM((N, 16, D), bf16)
    piece = pltpu.VMEM((N, 16, HALF_D), bf16)
    one = pltpu.VMEM((16, HALF_D), bf16)
    weight = pltpu.VMEM((D, K), bf16)
    image = pltpu.VMEM((128, D), bf16)
    four = pltpu.VMEM((4, 2, 16, D), bf16)
    scratch = [
        image, image, pltpu.VMEM((64, D), bf16), weight, weight,
        block, block, block, pltpu.VMEM((N, N, 16, D), bf16),
        pltpu.VMEM((512, D), bf16), pltpu.VMEM((512, D), bf16),
        pltpu.VMEM((4, 4, 2, 2, 16, D), bf16), pltpu.VMEM((4, 4, 2, 16, D), bf16),
        pltpu.VMEM((4, 3, 2, 16, D), bf16), four, four, four,
        block, block, block, block,
        piece, piece, one, piece, one, piece, one, pltpu.VMEM((4, 16, HALF_D), bf16),
        pltpu.VMEM((512, K), bf16), pltpu.VMEM((512, K), bf16),
        image, pltpu.VMEM((64, 320), f32), weight, weight,
        pltpu.SemaphoreType.DMA((9,)),
        pltpu.SemaphoreType.DMA((N_SEMS,)),
        pltpu.SemaphoreType.DMA((N_SEMS,)),
    ]
    anywhere = pl.BlockSpec(memory_space=pl.ANY)
    shapes = (
        jax.ShapeDtypeStruct((128, D), bf16),
        jax.ShapeDtypeStruct((64, 320), f32),
        jax.ShapeDtypeStruct((D, K), bf16),
        jax.ShapeDtypeStruct((D, K), bf16),
    )
    made = pl.pallas_call(
        kernel,
        out_shape=shapes,
        in_specs=[anywhere] * 5,
        out_specs=(anywhere,) * 4,
        scratch_shapes=scratch,
        compiler_params=pltpu.CompilerParams(
            collective_id=0, has_side_effects=True, vmem_limit_bytes=56 * 2**20
        ),
        cost_estimate=pl.CostEstimate(flops=4 * 10**9, bytes_accessed=6 * 10**6, transcendentals=500000),
    )(tokens[0], grad_out[0], router.T, up_weight[0], down_weight[0])
    gx, gr, gu, gd = pl.pallas_call(
        keep,
        out_shape=shapes,
        in_specs=[anywhere] * 4,
        out_specs=(anywhere,) * 4,
        scratch_shapes=[
            image, pltpu.VMEM((64, 320), f32), weight, weight, pltpu.SemaphoreType.DMA((2, 4, 2))
        ],
        compiler_params=pltpu.CompilerParams(vmem_limit_bytes=56 * 2**20),
    )(*made)
    return (gx[None], gr.T, gu[None], gd[None])


def solution(mesh):
    placed = (
        P(("expert", "dp"), None, None),
        P(("expert", "dp"), None, None),
        P(),
        P("expert", None, "dp"),
        P("expert", None, "dp"),
    )
    return jax.shard_map(
        local,
        mesh=mesh,
        in_specs=placed,
        out_specs=(
            P(("expert", "dp"), None, None),
            P("dp", None),
            P("expert", None, "dp"),
            P("expert", None, "dp"),
        ),
        check_vma=False,
    )
```

```python
import functools

import jax
import jax.numpy as jnp
from jax import lax
from jax.experimental import pallas as pl
from jax.experimental.pallas import tpu as pltpu
from jax.sharding import PartitionSpec as P

logit_scale = 24.0
f32 = jnp.float32
bf16 = jnp.bfloat16
MESH = pl.DeviceIdType.MESH
N = 8
D = 1280
K = 384
HALF_D = 640
ORDER = 'A3A2A1B3C3A0B2C2D3B1C1E3D2B0C0E2D1G3E1D0G2E0G1G0'


def dot(a, b, ca, cb):
    return lax.dot_general(a, b, (((ca,), (cb,)), ((), ())), preferred_element_type=f32)


def bits(m):
    return m // 4, (m // 2) % 2, m % 2


def flip(bit, by):
    return 1 - bit if by else bit


def step(g, dz, dx, dy):
    z, x, y = g // 16, (g // 4) % 4, g % 4
    return ((z + dz) % 4) * 16 + ((x + dx) % 4) * 4 + (y + dy) % 4


def receiver(g, m, j):
    yl, zl, c = bits(m)
    b, odd, dx1 = j // 4, 1 - (j // 2) % 2, j % 2
    dx0 = c * b + (1 - c) * flip(yl, b)
    dy = c * (3 - 2 * yl) + (1 - c) * 2 * b
    dz = 3 - 2 * zl if odd else 2 * flip(zl, dx1)
    to_y = c * (1 - yl) + (1 - c) * flip(yl, b)
    to_z = 1 - zl if odd else dx1
    i = b * 4 + (1 - odd) * 2 + flip(zl, dx1)
    return step(g, dz, dx1 * 2 + dx0, dy), to_y * 4 + to_z * 2 + c, i


def sender(e, t, i):
    yl, zl, c = bits(t)
    b, odd, q = i // 4, 1 - (i // 2) % 2, i % 2
    dx1 = flip(1 - zl, q) if odd else zl
    dz = 1 + 2 * zl if odd else 2 * q
    dy = c * (1 + 2 * yl) + (1 - c) * 2 * b
    dx0 = c * b + (1 - c) * yl
    from_y = c * (1 - yl) + (1 - c) * flip(yl, b)
    from_z = 1 - zl if odd else flip(zl, q)
    j = b * 4 + (1 - odd) * 2 + dx1
    return step(e, 4 - dz, 4 - (dx1 * 2 + dx0), 4 - dy), from_y * 4 + from_z * 2 + c, j


SELF = 2


def by_expert(g):
    def source(o):
        h, e = o >> 6, o & 63
        dz = ((e >> 4) - g // 16) & 3
        dx = ((e >> 2) - g // 4) & 3
        dy = (e - g) & 3
        dx0, dx1, c, odd = dx & 1, dx >> 1, dy & 1, dz & 1
        yl = c * (1 - (dy >> 1)) + (1 - c) * ((dy >> 1) ^ dx0)
        zl = odd * (1 - (dz >> 1)) + (1 - odd) * ((dz >> 1) ^ dx1)
        b = c * dx0 + (1 - c) * (dy >> 1)
        j = b * 4 + (1 - odd) * 2 + dx1
        return (yl * 4 + zl * 2 + c) * 16 + h * 8 + j

    return source


def pick(source, inverse=False):
    rows = lax.broadcasted_iota(jnp.int32, (128, 128), 0)
    cols = lax.broadcasted_iota(jnp.int32, (128, 128), 1)
    hit = rows == source(cols) if inverse else source(rows) == cols
    return jnp.where(hit, 1.0, 0.0).astype(bf16)


def swapped(o):
    return (o & 7) * 16 + ((o >> 3) & 1) * 8 + (o >> 4)


def moved(one_hot, value):
    return dot(one_hot, value, 1, 0).astype(bf16)


def to_row(column):
    return jnp.broadcast_to(column, (128, 128)).T[0:1, :]


def to_column(row):
    return jnp.broadcast_to(row, (128, 128)).T[:, 0:1]


def front(x, go, rt):
    xf = x.astype(f32)
    rf = rt.astype(f32)
    inv_x = to_row(lax.rsqrt(jnp.sum(xf * xf, axis=1, keepdims=True) + 1e-06))
    inv_r = lax.rsqrt(jnp.sum(rf * rf, axis=1, keepdims=True) + 1e-06)
    logits = (logit_scale * inv_x) * inv_r * dot(rt, x, 1, 1)
    e = jnp.exp(logits)
    disp = e / jnp.sum(e, axis=1, keepdims=True)
    comb = e / jnp.sum(e, axis=0, keepdims=True)
    slots = dot(disp.astype(bf16), x, 1, 0).astype(bf16)
    grads = dot(comb.astype(bf16), go, 1, 0).astype(bf16)
    return inv_x, inv_r, logits, disp, comb, slots, grads


def back(x, go, rt, saved, slots_out, grad_slots):
    inv_x, inv_r, logits, disp, comb = saved
    d_comb = dot(slots_out, go, 1, 1).astype(bf16).astype(f32)
    d_disp = dot(grad_slots, x, 1, 1).astype(bf16).astype(f32)
    d_log = disp * (d_disp - jnp.sum(disp * d_disp, axis=1, keepdims=True)) + comb * (
        d_comb - jnp.sum(comb * d_comb, axis=0, keepdims=True)
    )
    m = d_log * logits
    row = jnp.sum(m, axis=0, keepdims=True)
    col = jnp.sum(m, axis=1, keepdims=True)
    a = (logit_scale * inv_x) * inv_r * d_log
    hi = a.astype(bf16)
    lo = (a - hi.astype(f32)).astype(bf16)
    term = dot(jnp.concatenate([hi, lo], axis=0), x, 1, 0)
    term = term[:64] + term[64:] - rt.astype(f32) * (inv_r * inv_r * col)
    return hi, lo, row, term


def kernel(
    x_hbm, go_hbm, rt_hbm, wu_hbm, wd_hbm, gx_hbm, gr_hbm, gu_hbm, gd_hbm,
    x_ref, go_ref, rt_ref, wu_ref, wd_ref,
    s1, r1, s2, xg, xs, gs, parts, sibr, cs, rel, fy, fz, s3, r3, s4, r4,
    tp, q1, t2, q2, t3, q3, t4, ro, act_ref, dpre_ref, gx, gr, gu, gd, to_members, to_experts, swap,
    lsem, ssem, rsem,
):
    loads = [
        pltpu.make_async_copy(a, b, lsem.at[i])
        for i, (a, b) in enumerate(
            [(x_hbm, x_ref), (rt_hbm, rt_ref), (go_hbm, go_ref), (wu_hbm, wu_ref), (wd_hbm, wd_ref)]
        )
    ]
    for c in loads[:3]:
        c.start()

    ex, dp = lax.axis_index("expert"), lax.axis_index("dp")
    G, M = ex // 2, (ex % 2) * 4 + dp

    def dev(g, m):
        return {"expert": 2 * g + m // 4, "dp": m % 4}

    group = [(G, (M + d) % N) for d in range(1, N)]
    outs = [receiver(G, M, j) for j in range(N)]
    ins = [sender(G, M, i) for i in range(N)]
    far = [(G % N + N * ((G // N + d) % N), M) for d in range(1, N)]
    near = [((G // N) * N + (G % N + d) % N, M) for d in range(1, N)]
    keeps = M == 0

    barrier = pltpu.get_barrier_semaphore()

    def greet(g, m):
        pl.semaphore_signal(barrier, inc=1, device_id=dev(g, m), device_id_type=MESH)

    for g, m in group:
        greet(g, m)
    for n in range(N):
        for g, m, _ in (ins[n],):
            if n == SELF:
                pl.when(jnp.logical_not(keeps))(functools.partial(greet, g, m))
            else:
                greet(g, m)

    sems = [0]
    pending = []

    def sems_of(n):
        at = sems[0]
        sems[0] += n
        return at

    def copy(src, dst, s, r, to):
        return pltpu.make_async_remote_copy(
            src_ref=src, dst_ref=dst, send_sem=ssem.at[s], recv_sem=rsem.at[r],
            device_id=dev(*to), device_id_type=MESH,
        )

    def all_to_all(src, dst):
        at = sems_of(N - 1)
        for d in range(1, N):
            to = (G, (M + d) % N)
            c = copy(src.at[to[1]], dst.at[M], at + d - 1, at + d - 1, to)
            c.start()
            pending.append((c, None))
        dst[M] = src[M]

        def wait():
            for d in range(1, N):
                came = (M - d + N) % N
                copy(src.at[came], dst.at[came], at + d - 1, at + d - 1, (G, came)).wait_recv()

        return wait

    def exchange(src, dst, partners, slot, n):
        at = sems_of(n - 1)
        for d in range(1, n):
            c = copy(src, dst.at[slot], at + d - 1, at + d - 1, partners[d - 1])
            c.start()
            pending.append((c, None))
        dst[slot] = src[...]
        drain(n - 1)
        for d in range(1, n):
            came = (slot - d + n) % n
            copy(src, dst.at[came], at + d - 1, at + d - 1, partners[d - 1]).wait_recv()

    def unless(me, do):
        if me is None:
            do()
        else:
            pl.when(jnp.logical_not(me))(do)

    def cross_send(at, n, src, dst, own, to):
        c = copy(src, dst, at + n, at + to[2], to[:2])
        me = keeps if n == SELF else None
        unless(me, c.start)
        if me is not None:

            @pl.when(me)
            def _():
                own[...] = src[...]

        pending.append((c, me))

    def cross_wait(at, n, dst, source):
        unless(keeps if n == SELF else None, copy(dst, dst, at + n, at + n, source[:2]).wait_recv)

    def drain(keep):
        while len(pending) > keep:
            c, me = pending.pop(0)
            unless(me, c.wait_send)

    def send(src, dst, to):
        at = sems_of(1)
        c = copy(src, dst, at, at, to)
        c.start()
        pending.append((c, None))
        return c

    to_members[...] = pick(by_expert(G), inverse=True)
    to_experts[...] = pick(by_expert(G))
    swap[...] = pick(swapped)
    for c in loads[:3]:
        c.wait()
    for c in loads[3:]:
        c.start()
    x, go, rt = x_ref[...], go_ref[...], rt_ref[...]
    *saved, slots, grads = front(x, go, rt)
    slotted = jnp.concatenate([slots, grads], axis=0)
    s1[...] = moved(to_members[...], slotted).reshape(N, 16, D)
    pl.semaphore_wait(barrier, 7 + 8 - (1 - jnp.minimum(M, 1)))

    all_to_all(s1, r1)()
    s2[...] = moved(swap[...], r1[...].reshape(128, D)).reshape(N, 16, D)
    at2, at3 = sems_of(N), sems_of(N)
    for j in (6, 7, 4, 5, 2, 3, 0, 1):
        g, t, i = outs[j]
        cross_send(at2, j, s2.at[j], xg.at[t, i], xg.at[M, SELF], outs[j])

    yl, zl, c0 = bits(M)
    my, mz, md = M + 4 - 8 * yl, M + 2 - 4 * zl, 7 - M + 2 * c0 - 1
    ms = 1 - 2 * c0
    chip, chip_y, chip_z, chip_d = M // 2, my // 2, mz // 2, md // 2
    Y, Z, S = (G, my), (G, mz), (G, M + ms)
    marks = {}

    def rows_of(m, q):
        return xg.at[m, pl.ds(2 * q, 2)]

    def spread(m, q, name, to):
        marks[name, q] = send(rows_of(m, q), rows_of(m, q), to)

    O = (G, md)

    def stage_a(q):
        for i in (2 * q, 2 * q + 1):
            cross_wait(at2, i, xg.at[M, i], ins[i])
        spread(M, q, "s", S)
        spread(M, q, "d", O)
        spread(M, q, "y", Y)
        spread(M, q, "z", Z)

    def stage_b(q):
        marks["y", q].wait_recv()
        spread(my, q, "sy", S)
        marks["z", q].wait_recv()
        spread(mz, q, "sz", S)

    def stage_c(q):
        marks["d", q].wait_recv()
        spread(md, q, "sd", S)

    def stage_d(q):
        for name in ("s", "sy", "sz", "sd"):
            marks[name, q].wait_recv()
        if str(q) == ORDER[ORDER.index("D") + 1]:
            loads[3].wait()
            loads[4].wait()
        wu, wd = wu_ref[...], wd_ref[...]
        both = xg[:, 2 * q : 2 * q + 2].astype(f32).reshape(16, 2, 8, D)
        rows = both[:, 0].reshape(128, D).astype(bf16)
        grows = both[:, 1].reshape(128, D).astype(bf16)
        at = slice(128 * q, 128 * q + 128)
        xs[at, :] = rows
        gs[at, :] = grows
        pre = dot(rows, wu, 1, 0)
        cdf = 0.5 * (1.0 + lax.erf(pre * 0.7071067811865476))
        pdf = 0.3989422804014327 * jnp.exp(-0.5 * pre * pre)
        act = (pre * cdf).astype(bf16)
        dpre = (dot(grows, wd, 1, 0) * (cdf + pre * pdf)).astype(bf16)
        act_ref[at, :] = act
        dpre_ref[at, :] = dpre
        out = dot(act, wd, 1, 1).reshape(16, 1, 8, D)
        back_out = dot(dpre, wu, 1, 1).reshape(16, 1, 8, D)
        mixed = jnp.concatenate([out, back_out], axis=1).reshape(16, 16, D).astype(bf16)
        parts[q] = mixed.reshape(4, 2, 2, 16, D)
        marks["p", q] = send(parts.at[q, :, 1 - c0], sibr.at[q], S)

    def chip_sum(q, to):
        return parts[q, to, c0].astype(f32) + sibr[q, to].astype(f32)

    def forward(q, n, value, dst, name, to):
        cs[q, n] = value.astype(bf16)
        marks[name, q] = send(cs.at[q, n], dst.at[q], to)

    def stage_e(q):
        marks["p", q].wait_recv()
        forward(q, 0, chip_sum(q, chip_d), rel, "r", O)
        forward(q, 1, chip_sum(q, chip_z), fz, "fz", Z)
        forward(q, 2, chip_sum(q, chip_y), fy, "fy", Y)

    def stage_g(q):
        for name in ("fy", "fz", "r"):
            marks[name, q].wait_recv()
        total = chip_sum(q, chip) + fy[q].astype(f32) + fz[q].astype(f32) + rel[q].astype(f32)
        s3[2 * q : 2 * q + 2] = total.astype(bf16)
        for i in (2 * q + 1, 2 * q):
            g, t, j = ins[i]
            cross_send(at3, i, s3.at[i], r3.at[j], r3.at[SELF], ins[i])

    stages = {"A": stage_a, "B": stage_b, "C": stage_c, "D": stage_d, "E": stage_e, "G": stage_g}
    for n in range(len(ORDER) // 2):
        stages[ORDER[2 * n]](int(ORDER[2 * n + 1]))

    gd[...] = dot(gs[...], act_ref[...], 0, 0).astype(bf16)
    stores = [pltpu.make_async_copy(gd, gd_hbm, lsem.at[6])]
    stores[0].start()

    drain(8)

    for j in range(N):
        cross_wait(at3, j, r3.at[j], outs[j])
    s4[...] = moved(swap[...], r3[...].reshape(128, D)).reshape(N, 16, D)
    wait = all_to_all(s4, r4)
    gu[...] = dot(xs[...], dpre_ref[...], 0, 0).astype(bf16)
    stores.append(pltpu.make_async_copy(gu, gu_hbm, lsem.at[5]))
    stores[1].start()
    drain(7)
    wait()
    got = moved(to_experts[...], r4[...].reshape(128, D))
    slots_out, grad_slots = got[:64], got[64:]
    x, go, rt = x_ref[...], go_ref[...], rt_ref[...]
    hi, lo, row, term = back(x, go, rt, saved, slots_out, grad_slots)

    tb = term.astype(bf16)
    for m in range(N):
        r, zh = (m // 4) * 2 + m % 2, (m // 2) % 2
        tp[m] = tb[16 * r : 16 * r + 16, HALF_D * zh : HALF_D * (zh + 1)]
    wait = all_to_all(tp, q1)

    left = jnp.concatenate([saved[3].astype(bf16), hi, lo], axis=0)
    right = jnp.concatenate([grad_slots, rt, rt], axis=0)
    inv_x = saved[0]
    gx[...] = (dot(left, right, 0, 0) - x.astype(f32) * to_column(inv_x * inv_x * row)).astype(bf16)
    stores.append(pltpu.make_async_copy(gx, gx_hbm, lsem.at[7]))
    stores[2].start()
    wait()
    t2[...] = jnp.sum(q1[...].astype(f32), axis=0).astype(bf16)
    exchange(t2, q2, far, G // N, N)
    t3[...] = jnp.sum(q2[...].astype(f32), axis=0).astype(bf16)
    exchange(t3, q3, near, G % N, N)
    t4[...] = jnp.sum(q3[...].astype(f32), axis=0).astype(bf16)
    r = yl * 2 + c0
    same = [(r + d) % 4 for d in range(1, 4)]
    exchange(t4, ro, [(G, (a // 2) * 4 + zl * 2 + a % 2) for a in same], r, 4)
    whole = ro[...].reshape(64, HALF_D).astype(f32)
    gr[...] = jnp.where(c0 == 0, whole[:, :320], whole[:, 320:])
    stores.append(pltpu.make_async_copy(gr, gr_hbm, lsem.at[8]))
    stores[3].start()

    drain(0)
    for c in stores:
        c.wait()


def keep(*refs):
    ins, outs, bufs, sem = refs[:4], refs[4:8], refs[8:12], refs[12]
    parts = [(n, h) for n in (2, 3, 0, 1) for h in (0, 1)]

    def part(ref, h):
        half = ref.shape[0] // 2
        return ref.at[pl.ds(h * half, half)]

    reads = [
        pltpu.make_async_copy(part(ins[n], h), part(bufs[n], h), sem.at[0, n, h]) for n, h in parts
    ]
    writes = [
        pltpu.make_async_copy(part(bufs[n], h), part(outs[n], h), sem.at[1, n, h]) for n, h in parts
    ]
    for one in reads:
        one.start()
    for one, two in zip(reads, writes):
        one.wait()
        two.start()
    for two in writes:
        two.wait()


N_SEMS = 7 + 8 + 8 + 4 * (7 + 4) + 7 + 7 + 7 + 7 + 3


def local(tokens, grad_out, router, up_weight, down_weight):
    block = pltpu.VMEM((N, 16, D), bf16)
    piece = pltpu.VMEM((N, 16, HALF_D), bf16)
    one = pltpu.VMEM((16, HALF_D), bf16)
    weight = pltpu.VMEM((D, K), bf16)
    image = pltpu.VMEM((128, D), bf16)
    four = pltpu.VMEM((4, 2, 16, D), bf16)
    moves = pltpu.VMEM((128, 128), bf16)
    scratch = [
        image, image, pltpu.VMEM((64, D), bf16), weight, weight,
        block, block, block, pltpu.VMEM((N, N, 16, D), bf16),
        pltpu.VMEM((512, D), bf16), pltpu.VMEM((512, D), bf16),
        pltpu.VMEM((4, 4, 2, 2, 16, D), bf16), pltpu.VMEM((4, 4, 2, 16, D), bf16),
        pltpu.VMEM((4, 3, 2, 16, D), bf16), four, four, four,
        block, block, block, block,
        piece, piece, one, piece, one, piece, one, pltpu.VMEM((4, 16, HALF_D), bf16),
        pltpu.VMEM((512, K), bf16), pltpu.VMEM((512, K), bf16),
        image, pltpu.VMEM((64, 320), f32), weight, weight, moves, moves, moves,
        pltpu.SemaphoreType.DMA((9,)),
        pltpu.SemaphoreType.DMA((N_SEMS,)),
        pltpu.SemaphoreType.DMA((N_SEMS,)),
    ]
    anywhere = pl.BlockSpec(memory_space=pl.ANY)
    shapes = (
        jax.ShapeDtypeStruct((128, D), bf16),
        jax.ShapeDtypeStruct((64, 320), f32),
        jax.ShapeDtypeStruct((D, K), bf16),
        jax.ShapeDtypeStruct((D, K), bf16),
    )
    made = pl.pallas_call(
        kernel,
        out_shape=shapes,
        in_specs=[anywhere] * 5,
        out_specs=(anywhere,) * 4,
        scratch_shapes=scratch,
        compiler_params=pltpu.CompilerParams(
            collective_id=0, has_side_effects=True, vmem_limit_bytes=56 * 2**20
        ),
        cost_estimate=pl.CostEstimate(flops=4 * 10**9, bytes_accessed=6 * 10**6, transcendentals=500000),
    )(tokens[0], grad_out[0], router.T, up_weight[0], down_weight[0])
    gx, gr, gu, gd = pl.pallas_call(
        keep,
        out_shape=shapes,
        in_specs=[anywhere] * 4,
        out_specs=(anywhere,) * 4,
        scratch_shapes=[
            image, pltpu.VMEM((64, 320), f32), weight, weight, pltpu.SemaphoreType.DMA((2, 4, 2))
        ],
        compiler_params=pltpu.CompilerParams(vmem_limit_bytes=56 * 2**20),
    )(*made)
    return (gx[None], gr.T, gu[None], gd[None])


def solution(mesh):
    placed = (
        P(("expert", "dp"), None, None),
        P(("expert", "dp"), None, None),
        P(),
        P("expert", None, "dp"),
        P("expert", None, "dp"),
    )
    return jax.shard_map(
        local,
        mesh=mesh,
        in_specs=placed,
        out_specs=(
            P(("expert", "dp"), None, None),
            P("dp", None),
            P("expert", None, "dp"),
            P("expert", None, "dp"),
        ),
        check_vma=False,
    )
```

```python
import functools

import jax
import jax.numpy as jnp
from jax import lax
from jax.experimental import pallas as pl
from jax.experimental.pallas import tpu as pltpu
from jax.sharding import PartitionSpec as P

logit_scale = 24.0
f32 = jnp.float32
bf16 = jnp.bfloat16
MESH = pl.DeviceIdType.MESH
N = 8
D = 1280
K = 384
HALF_D = 640
ORDER = 'A3A2A1B3C3A0B2C2D3B1C1E3D2B0C0E2D1G3E1D0G2E0G1G0'


def dot(a, b, ca, cb):
    return lax.dot_general(a, b, (((ca,), (cb,)), ((), ())), preferred_element_type=f32)


def bits(m):
    return m // 4, (m // 2) % 2, m % 2


def flip(bit, by):
    return 1 - bit if by else bit


def step(g, dz, dx, dy):
    z, x, y = g // 16, (g // 4) % 4, g % 4
    return ((z + dz) % 4) * 16 + ((x + dx) % 4) * 4 + (y + dy) % 4


def receiver(g, m, j):
    yl, zl, c = bits(m)
    b, odd, dx1 = j // 4, 1 - (j // 2) % 2, j % 2
    dx0 = c * b + (1 - c) * flip(yl, b)
    dy = c * (3 - 2 * yl) + (1 - c) * 2 * b
    dz = 3 - 2 * zl if odd else 2 * flip(zl, dx1)
    to_y = c * (1 - yl) + (1 - c) * flip(yl, b)
    to_z = 1 - zl if odd else dx1
    i = b * 4 + (1 - odd) * 2 + flip(zl, dx1)
    return step(g, dz, dx1 * 2 + dx0, dy), to_y * 4 + to_z * 2 + c, i


def sender(e, t, i):
    yl, zl, c = bits(t)
    b, odd, q = i // 4, 1 - (i // 2) % 2, i % 2
    dx1 = flip(1 - zl, q) if odd else zl
    dz = 1 + 2 * zl if odd else 2 * q
    dy = c * (1 + 2 * yl) + (1 - c) * 2 * b
    dx0 = c * b + (1 - c) * yl
    from_y = c * (1 - yl) + (1 - c) * flip(yl, b)
    from_z = 1 - zl if odd else flip(zl, q)
    j = b * 4 + (1 - odd) * 2 + dx1
    return step(e, 4 - dz, 4 - (dx1 * 2 + dx0), 4 - dy), from_y * 4 + from_z * 2 + c, j


SELF = 2


def by_expert(g):
    def source(o):
        h, e = o >> 6, o & 63
        dz = ((e >> 4) - g // 16) & 3
        dx = ((e >> 2) - g // 4) & 3
        dy = (e - g) & 3
        dx0, dx1, c, odd = dx & 1, dx >> 1, dy & 1, dz & 1
        yl = c * (1 - (dy >> 1)) + (1 - c) * ((dy >> 1) ^ dx0)
        zl = odd * (1 - (dz >> 1)) + (1 - odd) * ((dz >> 1) ^ dx1)
        b = c * dx0 + (1 - c) * (dy >> 1)
        j = b * 4 + (1 - odd) * 2 + dx1
        return (yl * 4 + zl * 2 + c) * 16 + h * 8 + j

    return source


def pick(source, inverse=False):
    rows = lax.broadcasted_iota(jnp.int32, (128, 128), 0)
    cols = lax.broadcasted_iota(jnp.int32, (128, 128), 1)
    hit = rows == source(cols) if inverse else source(rows) == cols
    return jnp.where(hit, 1.0, 0.0).astype(bf16)


def swapped(o):
    return (o & 7) * 16 + ((o >> 3) & 1) * 8 + (o >> 4)


def moved(one_hot, value):
    return dot(one_hot, value, 1, 0).astype(bf16)


def to_row(column):
    return jnp.broadcast_to(column, (128, 128)).T[0:1, :]


def to_column(row):
    return jnp.broadcast_to(row, (128, 128)).T[:, 0:1]


def front(x, go, rt):
    xf = x.astype(f32)
    rf = rt.astype(f32)
    inv_x = to_row(lax.rsqrt(jnp.sum(xf * xf, axis=1, keepdims=True) + 1e-06))
    inv_r = lax.rsqrt(jnp.sum(rf * rf, axis=1, keepdims=True) + 1e-06)
    logits = (logit_scale * inv_x) * inv_r * dot(rt, x, 1, 1)
    e = jnp.exp(logits)
    disp = e / jnp.sum(e, axis=1, keepdims=True)
    comb = e / jnp.sum(e, axis=0, keepdims=True)
    slots = dot(disp.astype(bf16), x, 1, 0).astype(bf16)
    grads = dot(comb.astype(bf16), go, 1, 0).astype(bf16)
    return inv_x, inv_r, logits, disp, comb, slots, grads


def back(x, go, rt, saved, slots_out, grad_slots):
    inv_x, inv_r, logits, disp, comb = saved
    d_comb = dot(slots_out, go, 1, 1).astype(bf16).astype(f32)
    d_disp = dot(grad_slots, x, 1, 1).astype(bf16).astype(f32)
    d_log = disp * (d_disp - jnp.sum(disp * d_disp, axis=1, keepdims=True)) + comb * (
        d_comb - jnp.sum(comb * d_comb, axis=0, keepdims=True)
    )
    m = d_log * logits
    row = jnp.sum(m, axis=0, keepdims=True)
    col = jnp.sum(m, axis=1, keepdims=True)
    a = (logit_scale * inv_x) * inv_r * d_log
    hi = a.astype(bf16)
    lo = (a - hi.astype(f32)).astype(bf16)
    term = dot(jnp.concatenate([hi, lo], axis=0), x, 1, 0)
    term = term[:64] + term[64:] - rt.astype(f32) * (inv_r * inv_r * col)
    return hi, lo, row, term


def kernel(
    x_hbm, go_hbm, rt_hbm, wu_hbm, wd_hbm, gx_hbm, gr_hbm, gu_hbm, gd_hbm,
    x_ref, go_ref, rt_ref, wu_ref, wd_ref,
    s1, r1, s2, xg, xs, gs, parts, sibr, cs, rel, fy, fz, s3, r3, s4, r4,
    tp, q1, t2, q2, t3, q3, t4, ro, act_ref, dpre_ref, gx, gr, gu, gd, to_members, to_experts, swap,
    lsem, ssem, rsem,
):
    loads = [
        pltpu.make_async_copy(a, b, lsem.at[i])
        for i, (a, b) in enumerate(
            [(x_hbm, x_ref), (rt_hbm, rt_ref), (go_hbm, go_ref), (wu_hbm, wu_ref), (wd_hbm, wd_ref)]
        )
    ]
    for c in loads[:3]:
        c.start()

    ex, dp = lax.axis_index("expert"), lax.axis_index("dp")
    G, M = ex // 2, (ex % 2) * 4 + dp

    def dev(g, m):
        return {"expert": 2 * g + m // 4, "dp": m % 4}

    group = [(G, (M + d) % N) for d in range(1, N)]
    outs = [receiver(G, M, j) for j in range(N)]
    ins = [sender(G, M, i) for i in range(N)]
    far = [(G % N + N * ((G // N + d) % N), M) for d in range(1, N)]
    near = [((G // N) * N + (G % N + d) % N, M) for d in range(1, N)]
    keeps = M == 0

    barrier = pltpu.get_barrier_semaphore()

    def greet(g, m):
        pl.semaphore_signal(barrier, inc=1, device_id=dev(g, m), device_id_type=MESH)

    for g, m in group:
        greet(g, m)
    for n in range(N):
        for g, m, _ in (ins[n],):
            if n == SELF:
                pl.when(jnp.logical_not(keeps))(functools.partial(greet, g, m))
            else:
                greet(g, m)

    sems = [0]
    pending = []

    def sems_of(n):
        at = sems[0]
        sems[0] += n
        return at

    def copy(src, dst, s, r, to):
        return pltpu.make_async_remote_copy(
            src_ref=src, dst_ref=dst, send_sem=ssem.at[s], recv_sem=rsem.at[r],
            device_id=dev(*to), device_id_type=MESH,
        )

    def all_to_all(src, dst):
        at = sems_of(N - 1)
        for d in range(1, N):
            to = (G, (M + d) % N)
            c = copy(src.at[to[1]], dst.at[M], at + d - 1, at + d - 1, to)
            c.start()
            pending.append((c, None))
        dst[M] = src[M]

        def wait():
            for d in range(1, N):
                came = (M - d + N) % N
                copy(src.at[came], dst.at[came], at + d - 1, at + d - 1, (G, came)).wait_recv()

        return wait

    def exchange(src, dst, partners, slot, n):
        at = sems_of(n - 1)
        for d in range(1, n):
            c = copy(src, dst.at[slot], at + d - 1, at + d - 1, partners[d - 1])
            c.start()
            pending.append((c, None))
        dst[slot] = src[...]
        drain(n - 1)
        for d in range(1, n):
            came = (slot - d + n) % n
            copy(src, dst.at[came], at + d - 1, at + d - 1, partners[d - 1]).wait_recv()

    def unless(me, do):
        if me is None:
            do()
        else:
            pl.when(jnp.logical_not(me))(do)

    def cross_send(at, n, src, dst, own, to):
        c = copy(src, dst, at + n, at + to[2], to[:2])
        me = keeps if n == SELF else None
        unless(me, c.start)
        if me is not None:

            @pl.when(me)
            def _():
                own[...] = src[...]

        pending.append((c, me))

    def cross_wait(at, n, dst, source):
        unless(keeps if n == SELF else None, copy(dst, dst, at + n, at + n, source[:2]).wait_recv)

    def drain(keep):
        while len(pending) > keep:
            c, me = pending.pop(0)
            unless(me, c.wait_send)

    def send(src, dst, to):
        at = sems_of(1)
        c = copy(src, dst, at, at, to)
        c.start()
        pending.append((c, None))
        return c

    to_members[...] = pick(by_expert(G), inverse=True)
    to_experts[...] = pick(by_expert(G))
    swap[...] = pick(swapped)
    for c in loads[:3]:
        c.wait()
    for c in loads[3:]:
        c.start()
    x, go, rt = x_ref[...], go_ref[...], rt_ref[...]
    *saved, slots, grads = front(x, go, rt)
    slotted = jnp.concatenate([slots, grads], axis=0)
    s1[...] = moved(to_members[...], slotted).reshape(N, 16, D)
    pl.semaphore_wait(barrier, 7 + 8 - (1 - jnp.minimum(M, 1)))

    all_to_all(s1, r1)()
    s2[...] = moved(swap[...], r1[...].reshape(128, D)).reshape(N, 16, D)
    at2, at3 = sems_of(N), sems_of(N)
    for j in (6, 7, 4, 5, 2, 3, 0, 1):
        g, t, i = outs[j]
        cross_send(at2, j, s2.at[j], xg.at[t, i], xg.at[M, SELF], outs[j])

    yl, zl, c0 = bits(M)
    my, mz, md = M + 4 - 8 * yl, M + 2 - 4 * zl, 7 - M + 2 * c0 - 1
    ms = 1 - 2 * c0
    chip, chip_y, chip_z, chip_d = M // 2, my // 2, mz // 2, md // 2
    Y, Z, S = (G, my), (G, mz), (G, M + ms)
    marks = {}

    def rows_of(m, q):
        return xg.at[m, pl.ds(2 * q, 2)]

    def spread(m, q, name, to):
        marks[name, q] = send(rows_of(m, q), rows_of(m, q), to)

    O = (G, md)

    def stage_a(q):
        for i in (2 * q, 2 * q + 1):
            cross_wait(at2, i, xg.at[M, i], ins[i])
        spread(M, q, "s", S)
        spread(M, q, "d", O)
        spread(M, q, "y", Y)
        spread(M, q, "z", Z)

    def stage_b(q):
        marks["y", q].wait_recv()
        spread(my, q, "sy", S)
        marks["z", q].wait_recv()
        spread(mz, q, "sz", S)

    def stage_c(q):
        marks["d", q].wait_recv()
        spread(md, q, "sd", S)

    def stage_d(q):
        for name in ("s", "sy", "sz", "sd"):
            marks[name, q].wait_recv()
        if str(q) == ORDER[ORDER.index("D") + 1]:
            loads[3].wait()
            loads[4].wait()
        wu, wd = wu_ref[...], wd_ref[...]
        both = xg[:, 2 * q : 2 * q + 2].astype(f32).reshape(16, 2, 8, D)
        rows = both[:, 0].reshape(128, D).astype(bf16)
        grows = both[:, 1].reshape(128, D).astype(bf16)
        at = slice(128 * q, 128 * q + 128)
        xs[at, :] = rows
        gs[at, :] = grows
        pre = dot(rows, wu, 1, 0)
        cdf = 0.5 * (1.0 + lax.erf(pre * 0.7071067811865476))
        pdf = 0.3989422804014327 * jnp.exp(-0.5 * pre * pre)
        act = (pre * cdf).astype(bf16)
        dpre = (dot(grows, wd, 1, 0) * (cdf + pre * pdf)).astype(bf16)
        act_ref[at, :] = act
        dpre_ref[at, :] = dpre
        out = dot(act, wd, 1, 1).reshape(16, 1, 8, D)
        back_out = dot(dpre, wu, 1, 1).reshape(16, 1, 8, D)
        mixed = jnp.concatenate([out, back_out], axis=1).reshape(16, 16, D).astype(bf16)
        parts[q] = mixed.reshape(4, 2, 2, 16, D)
        for name, to in (("pd", chip_d), ("pz", chip_z), ("py", chip_y), ("p", chip)):
            marks[name, q] = send(parts.at[q, to, 1 - c0], sibr.at[q, to], S)

    def chip_sum(q, to):
        return parts[q, to, c0].astype(f32) + sibr[q, to].astype(f32)

    def forward(q, n, value, dst, name, to):
        cs[q, n] = value.astype(bf16)
        marks[name, q] = send(cs.at[q, n], dst.at[q], to)

    def stage_e(q):
        marks["pd", q].wait_recv()
        forward(q, 0, chip_sum(q, chip_d), rel, "r", O)
        marks["pz", q].wait_recv()
        forward(q, 1, chip_sum(q, chip_z), fz, "fz", Z)
        marks["py", q].wait_recv()
        forward(q, 2, chip_sum(q, chip_y), fy, "fy", Y)

    def stage_g(q):
        for name in ("p", "fy", "fz", "r"):
            marks[name, q].wait_recv()
        total = chip_sum(q, chip) + fy[q].astype(f32) + fz[q].astype(f32) + rel[q].astype(f32)
        s3[2 * q : 2 * q + 2] = total.astype(bf16)
        for i in (2 * q + 1, 2 * q):
            g, t, j = ins[i]
            cross_send(at3, i, s3.at[i], r3.at[j], r3.at[SELF], ins[i])

    stages = {"A": stage_a, "B": stage_b, "C": stage_c, "D": stage_d, "E": stage_e, "G": stage_g}
    for n in range(len(ORDER) // 2):
        stages[ORDER[2 * n]](int(ORDER[2 * n + 1]))

    gd[...] = dot(gs[...], act_ref[...], 0, 0).astype(bf16)
    stores = [pltpu.make_async_copy(gd, gd_hbm, lsem.at[6])]
    stores[0].start()

    drain(8)

    for j in range(N):
        cross_wait(at3, j, r3.at[j], outs[j])
    s4[...] = moved(swap[...], r3[...].reshape(128, D)).reshape(N, 16, D)
    wait = all_to_all(s4, r4)
    gu[...] = dot(xs[...], dpre_ref[...], 0, 0).astype(bf16)
    stores.append(pltpu.make_async_copy(gu, gu_hbm, lsem.at[5]))
    stores[1].start()
    drain(7)
    wait()
    got = moved(to_experts[...], r4[...].reshape(128, D))
    slots_out, grad_slots = got[:64], got[64:]
    x, go, rt = x_ref[...], go_ref[...], rt_ref[...]
    hi, lo, row, term = back(x, go, rt, saved, slots_out, grad_slots)

    tb = term.astype(bf16)
    for m in range(N):
        r, zh = (m // 4) * 2 + m % 2, (m // 2) % 2
        tp[m] = tb[16 * r : 16 * r + 16, HALF_D * zh : HALF_D * (zh + 1)]
    wait = all_to_all(tp, q1)

    left = jnp.concatenate([saved[3].astype(bf16), hi, lo], axis=0)
    right = jnp.concatenate([grad_slots, rt, rt], axis=0)
    inv_x = saved[0]
    gx[...] = (dot(left, right, 0, 0) - x.astype(f32) * to_column(inv_x * inv_x * row)).astype(bf16)
    stores.append(pltpu.make_async_copy(gx, gx_hbm, lsem.at[7]))
    stores[2].start()
    wait()
    t2[...] = jnp.sum(q1[...].astype(f32), axis=0).astype(bf16)
    exchange(t2, q2, far, G // N, N)
    t3[...] = jnp.sum(q2[...].astype(f32), axis=0).astype(bf16)
    exchange(t3, q3, near, G % N, N)
    t4[...] = jnp.sum(q3[...].astype(f32), axis=0).astype(bf16)
    r = yl * 2 + c0
    same = [(r + d) % 4 for d in range(1, 4)]
    exchange(t4, ro, [(G, (a // 2) * 4 + zl * 2 + a % 2) for a in same], r, 4)
    whole = ro[...].reshape(64, HALF_D).astype(f32)
    gr[...] = jnp.where(c0 == 0, whole[:, :320], whole[:, 320:])
    stores.append(pltpu.make_async_copy(gr, gr_hbm, lsem.at[8]))
    stores[3].start()

    drain(0)
    for c in stores:
        c.wait()


def keep(*refs):
    ins, outs, bufs, sem = refs[:4], refs[4:8], refs[8:12], refs[12]
    parts = [(n, h) for n in (2, 3, 0, 1) for h in (0, 1)]

    def part(ref, h):
        half = ref.shape[0] // 2
        return ref.at[pl.ds(h * half, half)]

    reads = [
        pltpu.make_async_copy(part(ins[n], h), part(bufs[n], h), sem.at[0, n, h]) for n, h in parts
    ]
    writes = [
        pltpu.make_async_copy(part(bufs[n], h), part(outs[n], h), sem.at[1, n, h]) for n, h in parts
    ]
    for one in reads:
        one.start()
    for one, two in zip(reads, writes):
        one.wait()
        two.start()
    for two in writes:
        two.wait()


N_SEMS = 7 + 8 + 8 + 4 * (7 + 7) + 7 + 7 + 7 + 7 + 3


def local(tokens, grad_out, router, up_weight, down_weight):
    block = pltpu.VMEM((N, 16, D), bf16)
    piece = pltpu.VMEM((N, 16, HALF_D), bf16)
    one = pltpu.VMEM((16, HALF_D), bf16)
    weight = pltpu.VMEM((D, K), bf16)
    image = pltpu.VMEM((128, D), bf16)
    four = pltpu.VMEM((4, 2, 16, D), bf16)
    moves = pltpu.VMEM((128, 128), bf16)
    scratch = [
        image, image, pltpu.VMEM((64, D), bf16), weight, weight,
        block, block, block, pltpu.VMEM((N, N, 16, D), bf16),
        pltpu.VMEM((512, D), bf16), pltpu.VMEM((512, D), bf16),
        pltpu.VMEM((4, 4, 2, 2, 16, D), bf16), pltpu.VMEM((4, 4, 2, 16, D), bf16),
        pltpu.VMEM((4, 3, 2, 16, D), bf16), four, four, four,
        block, block, block, block,
        piece, piece, one, piece, one, piece, one, pltpu.VMEM((4, 16, HALF_D), bf16),
        pltpu.VMEM((512, K), bf16), pltpu.VMEM((512, K), bf16),
        image, pltpu.VMEM((64, 320), f32), weight, weight, moves, moves, moves,
        pltpu.SemaphoreType.DMA((9,)),
        pltpu.SemaphoreType.DMA((N_SEMS,)),
        pltpu.SemaphoreType.DMA((N_SEMS,)),
    ]
    anywhere = pl.BlockSpec(memory_space=pl.ANY)
    shapes = (
        jax.ShapeDtypeStruct((128, D), bf16),
        jax.ShapeDtypeStruct((64, 320), f32),
        jax.ShapeDtypeStruct((D, K), bf16),
        jax.ShapeDtypeStruct((D, K), bf16),
    )
    made = pl.pallas_call(
        kernel,
        out_shape=shapes,
        in_specs=[anywhere] * 5,
        out_specs=(anywhere,) * 4,
        scratch_shapes=scratch,
        compiler_params=pltpu.CompilerParams(
            collective_id=0, has_side_effects=True, vmem_limit_bytes=56 * 2**20
        ),
        cost_estimate=pl.CostEstimate(flops=4 * 10**9, bytes_accessed=6 * 10**6, transcendentals=500000),
    )(tokens[0], grad_out[0], router.T, up_weight[0], down_weight[0])
    gx, gr, gu, gd = pl.pallas_call(
        keep,
        out_shape=shapes,
        in_specs=[anywhere] * 4,
        out_specs=(anywhere,) * 4,
        scratch_shapes=[
            image, pltpu.VMEM((64, 320), f32), weight, weight, pltpu.SemaphoreType.DMA((2, 4, 2))
        ],
        compiler_params=pltpu.CompilerParams(vmem_limit_bytes=56 * 2**20),
    )(*made)
    return (gx[None], gr.T, gu[None], gd[None])


def solution(mesh):
    placed = (
        P(("expert", "dp"), None, None),
        P(("expert", "dp"), None, None),
        P(),
        P("expert", None, "dp"),
        P("expert", None, "dp"),
    )
    return jax.shard_map(
        local,
        mesh=mesh,
        in_specs=placed,
        out_specs=(
            P(("expert", "dp"), None, None),
            P("dp", None),
            P("expert", None, "dp"),
            P("expert", None, "dp"),
        ),
        check_vma=False,
    )
```
